256 devices in a mesh: dp: 32 (over z_hi, x, core), sect: 8 (over y, z_lo).
Axes of the slice: x: 4, y: 4, z: 8 (z_hi: 4, z_lo: 2; z = z_hi * 2 + z_lo), core: 2. Of those that a mesh axis runs over, the one named last changes fastest.
Arguments:
- latent: bfloat16 [32, 2, 32, 256, 128], P('dp', None, 'sect'), may hold values from -6 to 6
- target: bfloat16 [32, 2, 32, 256, 128], P('dp', None, 'sect'), may hold values from -6 to 6
- w_dec: bfloat16 [2, 3, 3, 128, 128], replicated, may hold values from -0.125 to 0.125
- w_disc: bfloat16 [3, 3, 128, 128], replicated, may hold values from -0.1875 to 0.1875
- w_head: float32 [128], replicated, may hold values from -4 to 4
- w_perc: bfloat16 [128, 128], replicated, may hold values from -0.5 to 0.5
Outputs:
- grad_dec: float32 [2, 3, 3, 128, 128], replicated
The draws below stay inside these ranges and needn't reach their ends.
All inputs are finite; a program needn't handle non-finite values.
Results may differ from the reference program's by a relative error of at most 0.00065.
Values may be sent and summed in bfloat16 or wider, within the bound.
A program may use at most 64 MiB of HBM per device.

```python
import jax
import jax.numpy as jnp
from jax import lax

CH = 128
FRAMES = 2
COLS = 256
CLIPS = 32
HEIGHT = 32


def shard_levels(key, dims, cuts, smallest, high):
    factor_of, own = 1.0, jax.random.fold_in(key, 6)
    for axis_at, parts in cuts:
        steps = jnp.exp(jax.random.uniform(jax.random.fold_in(own, axis_at), (parts,), jnp.float32, smallest / len(cuts), high / len(cuts)))
        factor_of = factor_of * jnp.repeat(steps, dims[axis_at] // parts).reshape([-1 if axis == axis_at else 1 for axis in range(len(dims))])
    return factor_of


def gaussian(key, shape, scale, bound, cuts=(), dtype=jnp.bfloat16):
    entries = scale * jax.random.normal(key, shape, jnp.float32)
    if cuts:
        entries = entries * shard_levels(key, shape, cuts, -0.22, 0.18)
    return jnp.clip(entries, -bound, bound).astype(dtype)


def setup_inputs(seed: int = 0) -> dict:
    seeds = jax.random.split(jax.random.key(seed), 7)
    return {
        "latent": gaussian(seeds[0], (CLIPS, FRAMES, HEIGHT, COLS, CH), 1.0, 6.0, ((0, 32), (2, 8))),
        "target": gaussian(seeds[1], (CLIPS, FRAMES, HEIGHT, COLS, CH), 1.0, 6.0, ((0, 32), (2, 8))),
        "w_dec": gaussian(seeds[2], (2, 3, 3, CH, CH), (18 * CH) ** -0.5, 0.125),
        "w_disc": gaussian(seeds[3], (3, 3, CH, CH), (9 * CH) ** -0.5, 0.1875),
        "w_head": gaussian(seeds[4], (CH,), 1.0, 4.0, (), jnp.float32),
        "w_perc": gaussian(seeds[5], (CH, CH), CH ** -0.5, 0.5),
    }


def slope(value):
    sig = jax.nn.sigmoid(value)
    return sig * (1.0 + value * (1.0 - sig))

def conv_taps(padded, weight, frames, rows, cols):
    total = None
    for k in range(weight.shape[0]):
        for i in range(3):
            for j in range(3):
                piece = padded[k:k + frames, i:i + rows, j:j + cols].reshape(-1, padded.shape[-1])
                term = jnp.dot(piece, weight[k, i, j], preferred_element_type=jnp.float32)
                total = term if total is None else total + term
    return total

def weight_taps(padded, grads, frames, rows, cols):
    outer = []
    for k in range(2):
        for i in range(3):
            for j in range(3):
                piece = padded[k:k + frames, i:i + rows, j:j + cols].reshape(-1, padded.shape[-1])
                outer.append(lax.dot_general(piece, grads, (((0,), (0,)), ((), ())), preferred_element_type=jnp.float32))
    return jnp.stack(outer).reshape(2, 3, 3, padded.shape[-1], grads.shape[-1])

def reference(latent, target, w_dec, w_disc, w_head, w_perc):
    chans = latent.shape[-1]
    frames, height, cols = (latent.shape[1], latent.shape[2], latent.shape[3])
    w_flip = jnp.flip(w_disc, (0, 1)).transpose(0, 1, 3, 2)

    def one_clip(carry, pair):
        clip, goal = pair
        padded = jnp.pad(clip, ((1, 0), (1, 1), (1, 1), (0, 0)))
        pre = conv_taps(padded, w_dec, frames, height, cols)
        recon = jax.nn.silu(pre).astype(jnp.bfloat16)
        recon_pad = jnp.pad(recon.reshape(frames, height, cols, chans), ((0, 0), (1, 1), (1, 1), (0, 0)))
        disc = conv_taps(recon_pad, w_disc[None], frames, height, cols)
        grad_disc = (-w_head * slope(disc)).astype(jnp.bfloat16)
        gd_pad = jnp.pad(grad_disc.reshape(frames, height, cols, chans), ((0, 0), (1, 1), (1, 1), (0, 0)))
        back_disc = conv_taps(gd_pad, w_flip[None], frames, height, cols)
        feats = jnp.dot(recon, w_perc, preferred_element_type=jnp.float32)
        grad_feat = (feats - goal.reshape(-1, chans).astype(jnp.float32)).astype(jnp.bfloat16)
        back_perc = jnp.dot(grad_feat, w_perc.T, preferred_element_type=jnp.float32)
        grad_pre = ((back_disc + back_perc) * slope(pre)).astype(jnp.bfloat16)
        return (carry + weight_taps(padded, grad_pre, frames, height, cols), None)
    start = jnp.zeros((2, 3, 3, chans, chans), jnp.float32)
    total, _ = lax.scan(one_clip, start, (latent, target))
    pixels = latent.shape[0] * frames * height * cols
    return total / jnp.sqrt(jnp.float32(pixels))
```

```python
import functools

import jax
import jax.numpy as jnp
from jax import lax
from jax.experimental import pallas as pl
from jax.experimental.pallas import tpu as pltpu
from jax.sharding import PartitionSpec as P

MESH = pl.DeviceIdType.MESH
F32 = jnp.float32
BF16 = jnp.bfloat16
FRAMES, ROWS, COLS, CH = 2, 4, 256, 128
NX, NY, NZ = 4, 4, 8
TAPS = 18
HALF = TAPS * CH // 2
PIECE = HALF // (NX * NY)


def slope(value):
    sig = jax.nn.sigmoid(value)
    return sig * (1.0 + value * (1.0 - sig))


def shifted(tile):
    at = lax.broadcasted_iota(jnp.int32, tile.shape, 0)
    before = jnp.where(at == 0, 0.0, pltpu.roll(tile, 1, 0))
    after = jnp.where(at == COLS - 1, 0.0, pltpu.roll(tile, COLS - 1, 0))
    return before.astype(BF16), tile.astype(BF16), after.astype(BF16)


def dot(a, b):
    return jnp.dot(a, b, preferred_element_type=F32)


def kernel(
    lat_hbm, tgt_hbm, wdec_hbm, wdisc_hbm, whead_ref, wperc_ref,
    out_ref,
    xs, x3, xt, tgt, wa, wd, wb, wdv, rec, rhalo, r3, g3, gf, slp, p3,
    buf, cin, red, r1, r2,
    lsem, hsend, hrecv, csend, crecv, s1, v1, s2, v2, s3, v3, s4, v4,
):
    dp, sect = lax.axis_index("dp"), lax.axis_index("sect")
    core, px = lax.rem(dp, 2), lax.rem(dp // 2, NX)
    py, pz = sect // 2, (dp // 8) * 2 + lax.rem(sect, 2)

    def at(x, y, z, c):
        return ((z // 2) * 8 + x * 2 + c, y * 2 + lax.rem(z, 2))

    other = at(px, py, pz, 1 - core)

    def plane(d):
        return at(lax.rem(px + d // NY, NX), lax.rem(py + d % NY, NY), pz, core)

    def line(d):
        return at(px, py, lax.rem(pz + d, NZ), core)

    up, down = (dp, sect - 1), (dp, sect + 1)
    has_up, has_down = sect > 0, sect < 2 * NY - 1

    bar = pltpu.get_barrier_semaphore()

    def greet(who):
        pl.semaphore_signal(bar, inc=1, device_id=who, device_id_type=MESH)

    @pl.when(has_up)
    def _():
        greet(up)

    @pl.when(has_down)
    def _():
        greet(down)

    greet(other)
    for d in range(1, NX * NY):
        greet(plane(d))
    for d in range(1, NZ):
        greet(line(d))

    loads = [
        pltpu.make_async_copy(lat_hbm, xs.at[:, pl.ds(2, ROWS)], lsem.at[0]),
        pltpu.make_async_copy(wdec_hbm.at[1], wa.at[:, pl.ds(0, CH)], lsem.at[1]),
        pltpu.make_async_copy(wdec_hbm.at[0], wa.at[:, pl.ds(CH, CH)], lsem.at[2]),
        pltpu.make_async_copy(wdisc_hbm, wdv, lsem.at[3]),
        pltpu.make_async_copy(tgt_hbm, tgt, lsem.at[4]),
    ]
    for cp in loads:
        cp.start()

    zrow = jnp.zeros((FRAMES, COLS, CH), BF16)

    @pl.when(jnp.logical_not(has_up))
    def _():
        xs[:, 0] = zrow
        xs[:, 1] = zrow
        rhalo[0] = zrow

    @pl.when(jnp.logical_not(has_down))
    def _():
        xs[:, 6] = zrow
        xs[:, 7] = zrow
        rhalo[1] = zrow

    def widen(dst, t, idx, tile):
        for j, piece in enumerate(shifted(tile)):
            dst[t, idx, :, j * CH:(j + 1) * CH] = piece

    def widen_x(row):
        for t in range(FRAMES):
            tile = xs[t, row + 2]
            widen(x3, t, row + 2, tile.astype(F32))
            if -1 <= row <= ROWS:
                xt[t, row + 1] = tile.T

    def around(src, t, idx):
        return jnp.concatenate([src[t, idx - 1], src[t, idx], src[t, idx + 1]], axis=1)

    def pre_rows(rows):
        first = dot(jnp.concatenate([around(x3, 0, r + 2) for r in rows], axis=0), wa[...])
        second = dot(jnp.concatenate([around(x3, 1, r + 2) for r in rows], axis=0), wa[:, :CH])
        for n, r in enumerate(rows):
            span = slice(n * COLS, (n + 1) * COLS)
            for t in range(FRAMES):
                pre = first[span, :CH] if t == 0 else first[span, CH:] + second[span]
                sig = jax.nn.sigmoid(pre)
                value = pre * sig
                if r < 0:
                    value = jnp.where(has_up, value, 0.0)
                elif r >= ROWS:
                    value = jnp.where(has_down, value, 0.0)
                else:
                    slp[t, r] = sig * (1.0 + pre * (1.0 - sig))
                widen(r3, t, r + 2, value)
                if r in (1, 2):
                    rec[2 - r, t] = value.astype(BF16)

    def disc_rows(rows):
        own = 0 <= rows[0] < ROWS
        lhs = jnp.concatenate([around(r3, t, r + 2) for r in rows for t in range(FRAMES)], axis=0)
        res = dot(lhs, wd[...] if own else wd[:, :CH])
        for n, (r, t) in enumerate([(r, t) for r in rows for t in range(FRAMES)]):
            span = slice(n * COLS, (n + 1) * COLS)
            grad = -whead_ref[...] * slope(res[span, :CH])
            if r < 0:
                grad = jnp.where(has_up, grad, 0.0)
            elif r >= ROWS:
                grad = jnp.where(has_down, grad, 0.0)
            else:
                gf[t, r] = (res[span, CH:] - tgt[t, r].astype(F32)).astype(BF16)
            widen(g3, t, r + 1, grad)

    def back_rows(rows):
        pairs = [(r, t) for r in rows for t in range(FRAMES)]
        lhs = jnp.concatenate(
            [jnp.concatenate([around(g3, t, r + 1), gf[t, r]], axis=1) for r, t in pairs], axis=0
        )
        res = dot(lhs, wb[...])
        for n, (r, t) in enumerate(pairs):
            grad = res[n * COLS:(n + 1) * COLS] * slp[t, r]
            for j, piece in enumerate(shifted(grad)):
                p3[t, r, :, (2 - j) * CH:(3 - j) * CH] = piece

    def weight_rows(rows, first):
        def left(t, r):
            return xt[t, r:r + 3].reshape(3 * CH, COLS)

        lhs0 = jnp.concatenate([left(0, r) for r in rows], axis=1)
        rhs1 = jnp.concatenate([p3[1, r] for r in rows], axis=0)
        k0 = dot(lhs0, rhs1)
        lhs1 = jnp.concatenate([lhs0] + [left(1, r) for r in rows], axis=1)
        rhs = jnp.concatenate([p3[0, r] for r in rows] + [rhs1], axis=0)
        k1 = dot(lhs1, rhs)
        for k, res in enumerate((k0, k1)):
            for i in range(3):
                for j in range(3):
                    piece = res[i * CH:(i + 1) * CH, j * CH:(j + 1) * CH]
                    span = pl.ds(((k * 3 + i) * 3 + j) * CH, CH)
                    if first:
                        buf[span] = piece
                    else:
                        buf[span] += piece

    loads[0].wait()
    for row in range(ROWS):
        widen_x(row)
    loads[1].wait()
    loads[2].wait()
    pre_rows((1, 2))

    pl.semaphore_wait(bar, NX * NY - 1 + NZ - 1 + 1 + has_up.astype(jnp.int32) + has_down.astype(jnp.int32))

    def halo(n, src, dst, who):
        return pltpu.make_async_remote_copy(
            src_ref=src, dst_ref=dst, send_sem=hsend.at[n], recv_sem=hrecv.at[n],
            device_id=who, device_id_type=MESH,
        )

    halos = [
        halo(0, lat_hbm.at[:, 0], xs.at[:, 6], up),
        halo(1, lat_hbm.at[:, 3], xs.at[:, 1], down),
        halo(2, lat_hbm.at[:, 1], xs.at[:, 7], up),
        halo(3, lat_hbm.at[:, 2], xs.at[:, 0], down),
        halo(4, rec.at[1], rhalo.at[1], up),
        halo(5, rec.at[0], rhalo.at[0], down),
    ]

    @pl.when(has_up)
    def _():
        for n in (0, 2, 4):
            halos[n].start()

    @pl.when(has_down)
    def _():
        for n in (1, 3, 5):
            halos[n].start()

    def arrived(pair):
        @pl.when(has_down)
        def _():
            halos[2 * pair].wait_recv()

        @pl.when(has_up)
        def _():
            halos[2 * pair + 1].wait_recv()

    loads[3].wait()
    wd[:, :CH] = wdv[...]
    wd[:, CH:] = jnp.zeros((9 * CH, CH), BF16)
    wd[4 * CH:5 * CH, CH:] = wperc_ref[...]
    for tap in range(9):
        wb[tap * CH:(tap + 1) * CH] = wdv[(8 - tap) * CH:(9 - tap) * CH].T
    wb[9 * CH:] = wperc_ref[...].T
    loads[4].wait()

    arrived(0)
    widen_x(-1)
    widen_x(ROWS)
    pre_rows((0, 3))
    disc_rows((1, 2))

    arrived(1)
    widen_x(-2)
    widen_x(ROWS + 1)
    pre_rows((-1, ROWS))
    disc_rows((0, 3))
    back_rows((1, 2))
    weight_rows((1, 2), True)

    arrived(2)
    for side, row in ((0, -2), (1, ROWS + 1)):
        for t in range(FRAMES):
            widen(r3, t, row + 2, rhalo[side, t].astype(F32))
    disc_rows((-1, ROWS))
    back_rows((0, 3))
    weight_rows((0, 3), False)

    mine, theirs = core * HALF, (1 - core) * HALF
    swap = pltpu.make_async_remote_copy(
        src_ref=buf.at[pl.ds(theirs, HALF)], dst_ref=cin, send_sem=csend, recv_sem=crecv,
        device_id=other, device_id_type=MESH,
    )
    swap.start()
    swap.wait_recv()
    spot = px * NY + py
    scatter = []
    for d in range(1, NX * NY):
        q = lax.rem(px + d // NY, NX) * NY + lax.rem(py + d % NY, NY)
        rows = pl.ds(pl.multiple_of(q * PIECE, 8), PIECE)
        red[rows] = buf[pl.ds(pl.multiple_of(mine + q * PIECE, 8), PIECE)] + cin[rows]
        cp = pltpu.make_async_remote_copy(
            src_ref=red.at[rows], dst_ref=r1.at[spot], send_sem=s1.at[d], recv_sem=v1.at[d],
            device_id=plane(d), device_id_type=MESH,
        )
        cp.start()
        scatter.append(cp)
    own = pl.ds(pl.multiple_of(spot * PIECE, 8), PIECE)
    r1[spot] = buf[pl.ds(pl.multiple_of(mine + spot * PIECE, 8), PIECE)] + cin[own]
    for cp in scatter:
        cp.wait_recv()
    total = r1[0]
    for n in range(1, NX * NY):
        total = total + r1[n]
    r2[pz] = total
    spread = []
    for d in range(1, NZ):
        cp = pltpu.make_async_remote_copy(
            src_ref=r2.at[pz], dst_ref=r2.at[pz], send_sem=s2.at[d], recv_sem=v2.at[d],
            device_id=line(d), device_id_type=MESH,
        )
        cp.start()
        spread.append(cp)
    for cp in spread:
        cp.wait_recv()
    total = r2[0]
    for n in range(1, NZ):
        total = total + r2[n]
    own = pl.ds(pl.multiple_of(mine + spot * PIECE, 8), PIECE)
    out_ref[own] = total
    gather = []
    for d in range(1, NX * NY):
        cp = pltpu.make_async_remote_copy(
            src_ref=out_ref.at[own], dst_ref=out_ref.at[own], send_sem=s3.at[d], recv_sem=v3.at[d],
            device_id=plane(d), device_id_type=MESH,
        )
        cp.start()
        gather.append(cp)
    forward = []
    for d in range(NX * NY):
        q = lax.rem(px + NX - d // NY, NX) * NY + lax.rem(py + NY - d % NY, NY)
        if d:
            gather[d - 1].wait_recv()
        rows = pl.ds(pl.multiple_of(mine + q * PIECE, 8), PIECE)
        cp = pltpu.make_async_remote_copy(
            src_ref=out_ref.at[rows], dst_ref=out_ref.at[rows], send_sem=s4.at[d], recv_sem=v4.at[d],
            device_id=other, device_id_type=MESH,
        )
        cp.start()
        forward.append(cp)
    for cp in forward:
        cp.wait_recv()

    @pl.when(has_up)
    def _():
        for n in (0, 2, 4):
            halos[n].wait_send()

    @pl.when(has_down)
    def _():
        for n in (1, 3, 5):
            halos[n].wait_send()

    for cp in [swap] + scatter + spread + gather + forward:
        cp.wait_send()


def per_device(latent, target, w_dec, w_disc, w_head, w_perc):
    any_spec = pl.BlockSpec(memory_space=pl.ANY)
    vmem = pl.BlockSpec(memory_space=pltpu.VMEM)
    dma = pltpu.SemaphoreType.DMA
    plane, line = NX * NY, NZ
    total = pl.pallas_call(
        kernel,
        out_shape=jax.ShapeDtypeStruct((TAPS * CH, CH), F32),
        in_specs=[any_spec] * 4 + [vmem] * 2,
        out_specs=vmem,
        scratch_shapes=[
            pltpu.VMEM((FRAMES, ROWS + 4, COLS, CH), BF16),
            pltpu.VMEM((FRAMES, ROWS + 4, COLS, 3 * CH), BF16),
            pltpu.VMEM((FRAMES, ROWS + 2, CH, COLS), BF16),
            pltpu.VMEM((FRAMES, ROWS, COLS, CH), BF16),
            pltpu.VMEM((9 * CH, 2 * CH), BF16),
            pltpu.VMEM((9 * CH, 2 * CH), BF16),
            pltpu.VMEM((10 * CH, CH), BF16),
            pltpu.VMEM((9 * CH, CH), BF16),
            pltpu.VMEM((2, FRAMES, COLS, CH), BF16),
            pltpu.VMEM((2, FRAMES, COLS, CH), BF16),
            pltpu.VMEM((FRAMES, ROWS + 4, COLS, 3 * CH), BF16),
            pltpu.VMEM((FRAMES, ROWS + 2, COLS, 3 * CH), BF16),
            pltpu.VMEM((FRAMES, ROWS, COLS, CH), BF16),
            pltpu.VMEM((FRAMES, ROWS, COLS, CH), F32),
            pltpu.VMEM((FRAMES, ROWS, COLS, 3 * CH), BF16),
            pltpu.VMEM((TAPS * CH, CH), F32),
            pltpu.VMEM((HALF, CH), F32),
            pltpu.VMEM((HALF, CH), F32),
            pltpu.VMEM((plane, PIECE, CH), F32),
            pltpu.VMEM((line, PIECE, CH), F32),
            dma((5,)), dma((6,)), dma((6,)), dma, dma,
            dma((plane,)), dma((plane,)), dma((line,)), dma((line,)),
            dma((plane,)), dma((plane,)), dma((plane,)), dma((plane,)),
        ],
        compiler_params=pltpu.CompilerParams(
            collective_id=0, has_side_effects=True, vmem_limit_bytes=48 << 20
        ),
        name="tokenizer_step",
    )(
        latent[0], target[0], w_dec.reshape(2, 9 * CH, CH), w_disc.reshape(9 * CH, CH),
        w_head.reshape(1, CH), w_perc,
    )
    pixels = lax.axis_size("dp") * FRAMES * ROWS * lax.axis_size("sect") * COLS
    total = total / jnp.sqrt(jnp.float32(pixels))
    return total.reshape(2, 3, 3, CH, CH)


def solution(mesh):
    in_specs = (
        P("dp", None, "sect", None, None),
        P("dp", None, "sect", None, None),
        P(),
        P(),
        P(),
        P(),
    )
    return jax.shard_map(
        per_device, mesh=mesh, in_specs=in_specs, out_specs=P(), check_vma=False
    )
```

```python
import functools

import jax
import jax.numpy as jnp
from jax import lax
from jax.experimental import pallas as pl
from jax.experimental.pallas import tpu as pltpu
from jax.sharding import PartitionSpec as P

MESH = pl.DeviceIdType.MESH
F32 = jnp.float32
BF16 = jnp.bfloat16
FRAMES, ROWS, COLS, CH = 2, 4, 256, 128
NX, NY, NZ = 4, 4, 8
TAPS = 18
HALF = TAPS * CH // 2
PARTS = 3
PART = HALF // PARTS
PIECE = PART // (NX * NY)
PLANE = sorted(range(1, NX * NY), key=lambda d: -min(d // NY, NX - d // NY) - min(d % NY, NY - d % NY))
LINE = sorted(range(1, NZ), key=lambda d: -min(d, NZ - d))


def slope(value):
    sig = jax.nn.sigmoid(value)
    return sig * (1.0 + value * (1.0 - sig))


def shifted(tile):
    at = lax.broadcasted_iota(jnp.int32, tile.shape, 0)
    before = jnp.where(at == 0, 0.0, pltpu.roll(tile, 1, 0))
    after = jnp.where(at == COLS - 1, 0.0, pltpu.roll(tile, COLS - 1, 0))
    return before.astype(BF16), tile.astype(BF16), after.astype(BF16)


def dot(a, b):
    return jnp.dot(a, b, preferred_element_type=F32)


def kernel(
    lat_hbm, tgt_hbm, wdec_hbm, wdisc_hbm, whead_hbm, wperc_hbm,
    out_ref,
    xs, x3, xt, tgt, wa, wd, wb, wdv, whead_ref, wperc_ref, rec, rhalo, r3, g3, gf, slp, p3,
    buf, cin, red, r1, r2,
    lsem, hsend, hrecv, csend, crecv, s1, v1, s2, v2, s3, v3, s4, v4,
):
    dp, sect = lax.axis_index("dp"), lax.axis_index("sect")
    core, px = lax.rem(dp, 2), lax.rem(dp // 2, NX)
    py, pz = sect // 2, (dp // 8) * 2 + lax.rem(sect, 2)

    def at(x, y, z, c):
        return ((z // 2) * 8 + x * 2 + c, y * 2 + lax.rem(z, 2))

    other = at(px, py, pz, 1 - core)

    def plane(d):
        return at(lax.rem(px + d // NY, NX), lax.rem(py + d % NY, NY), pz, core)

    def line(d):
        return at(px, py, lax.rem(pz + d, NZ), core)

    up, down = (dp, sect - 1), (dp, sect + 1)
    has_up, has_down = sect > 0, sect < 2 * NY - 1

    bar = pltpu.get_barrier_semaphore()

    def greet(who):
        pl.semaphore_signal(bar, inc=1, device_id=who, device_id_type=MESH)

    @pl.when(has_up)
    def _():
        greet(up)

    @pl.when(has_down)
    def _():
        greet(down)

    greet(other)
    for d in range(1, NX * NY):
        greet(plane(d))
    for d in range(1, NZ):
        greet(line(d))

    loads = [
        pltpu.make_async_copy(lat_hbm, xs.at[:, pl.ds(2, ROWS)], lsem.at[0]),
        pltpu.make_async_copy(wdec_hbm.at[1], wa.at[:, pl.ds(0, CH)], lsem.at[1]),
        pltpu.make_async_copy(wdec_hbm.at[0], wa.at[:, pl.ds(CH, CH)], lsem.at[2]),
        pltpu.make_async_copy(wdisc_hbm, wdv, lsem.at[3]),
        pltpu.make_async_copy(wperc_hbm, wperc_ref, lsem.at[4]),
        pltpu.make_async_copy(whead_hbm, whead_ref, lsem.at[5]),
        pltpu.make_async_copy(tgt_hbm, tgt, lsem.at[6]),
    ]
    for cp in loads:
        cp.start()

    zrow = jnp.zeros((FRAMES, COLS, CH), BF16)

    @pl.when(jnp.logical_not(has_up))
    def _():
        xs[:, 0] = zrow
        xs[:, 1] = zrow
        rhalo[0] = zrow

    @pl.when(jnp.logical_not(has_down))
    def _():
        xs[:, 6] = zrow
        xs[:, 7] = zrow
        rhalo[1] = zrow

    def widen(dst, t, idx, tile):
        for j, piece in enumerate(shifted(tile)):
            dst[t, idx, :, j * CH:(j + 1) * CH] = piece

    def widen_x(row):
        for t in range(FRAMES):
            tile = xs[t, row + 2]
            widen(x3, t, row + 2, tile.astype(F32))
            if -1 <= row <= ROWS:
                xt[t, row + 1] = tile.T

    def around(src, t, idx):
        return jnp.concatenate([src[t, idx - 1], src[t, idx], src[t, idx + 1]], axis=1)

    def pre_rows(rows):
        first = dot(jnp.concatenate([around(x3, 0, r + 2) for r in rows], axis=0), wa[...])
        second = dot(jnp.concatenate([around(x3, 1, r + 2) for r in rows], axis=0), wa[:, :CH])
        for n, r in enumerate(rows):
            span = slice(n * COLS, (n + 1) * COLS)
            for t in range(FRAMES):
                pre = first[span, :CH] if t == 0 else first[span, CH:] + second[span]
                sig = jax.nn.sigmoid(pre)
                value = pre * sig
                if r < 0:
                    value = jnp.where(has_up, value, 0.0)
                elif r >= ROWS:
                    value = jnp.where(has_down, value, 0.0)
                else:
                    slp[t, r] = sig * (1.0 + pre * (1.0 - sig))
                widen(r3, t, r + 2, value)
                if r in (1, 2):
                    rec[2 - r, t] = value.astype(BF16)

    def disc_rows(rows):
        own = 0 <= rows[0] < ROWS
        lhs = jnp.concatenate([around(r3, t, r + 2) for r in rows for t in range(FRAMES)], axis=0)
        res = dot(lhs, wd[...] if own else wd[:, :CH])
        for n, (r, t) in enumerate([(r, t) for r in rows for t in range(FRAMES)]):
            span = slice(n * COLS, (n + 1) * COLS)
            grad = -whead_ref[...] * slope(res[span, :CH])
            if r < 0:
                grad = jnp.where(has_up, grad, 0.0)
            elif r >= ROWS:
                grad = jnp.where(has_down, grad, 0.0)
            else:
                gf[t, r] = (res[span, CH:] - tgt[t, r].astype(F32)).astype(BF16)
            widen(g3, t, r + 1, grad)

    def back_rows(rows):
        pairs = [(r, t) for r in rows for t in range(FRAMES)]
        lhs = jnp.concatenate(
            [jnp.concatenate([around(g3, t, r + 1), gf[t, r]], axis=1) for r, t in pairs], axis=0
        )
        res = dot(lhs, wb[...])
        for n, (r, t) in enumerate(pairs):
            grad = res[n * COLS:(n + 1) * COLS] * slp[t, r]
            for j, piece in enumerate(shifted(grad)):
                p3[t, r, :, (2 - j) * CH:(3 - j) * CH] = piece

    def weight_rows(rows, first):
        def left(t, r):
            return xt[t, r:r + 3].reshape(3 * CH, COLS)

        lhs0 = jnp.concatenate([left(0, r) for r in rows], axis=1)
        rhs1 = jnp.concatenate([p3[1, r] for r in rows], axis=0)
        k0 = dot(lhs0, rhs1)
        lhs1 = jnp.concatenate([lhs0] + [left(1, r) for r in rows], axis=1)
        rhs = jnp.concatenate([p3[0, r] for r in rows] + [rhs1], axis=0)
        k1 = dot(lhs1, rhs)
        for k, res in enumerate((k0, k1)):
            for i in range(3):
                for j in range(3):
                    piece = res[i * CH:(i + 1) * CH, j * CH:(j + 1) * CH]
                    span = pl.ds(((k * 3 + i) * 3 + j) * CH, CH)
                    if first:
                        buf[span] = piece
                    else:
                        buf[span] += piece

    loads[0].wait()
    for row in range(ROWS):
        widen_x(row)
    loads[1].wait()
    loads[2].wait()
    pre_rows((1, 2))

    pl.semaphore_wait(bar, NX * NY - 1 + NZ - 1 + 1 + has_up.astype(jnp.int32) + has_down.astype(jnp.int32))

    def halo(n, src, dst, who):
        return pltpu.make_async_remote_copy(
            src_ref=src, dst_ref=dst, send_sem=hsend.at[n], recv_sem=hrecv.at[n],
            device_id=who, device_id_type=MESH,
        )

    halos = [
        halo(0, lat_hbm.at[:, 0], xs.at[:, 6], up),
        halo(1, lat_hbm.at[:, 3], xs.at[:, 1], down),
        halo(2, lat_hbm.at[:, 1], xs.at[:, 7], up),
        halo(3, lat_hbm.at[:, 2], xs.at[:, 0], down),
        halo(4, rec.at[1], rhalo.at[1], up),
        halo(5, rec.at[0], rhalo.at[0], down),
    ]

    @pl.when(has_up)
    def _():
        for n in (0, 2, 4):
            halos[n].start()

    @pl.when(has_down)
    def _():
        for n in (1, 3, 5):
            halos[n].start()

    def arrived(pair):
        @pl.when(has_down)
        def _():
            halos[2 * pair].wait_recv()

        @pl.when(has_up)
        def _():
            halos[2 * pair + 1].wait_recv()

    loads[3].wait()
    loads[4].wait()
    wd[:, :CH] = wdv[...]
    wd[:, CH:] = jnp.zeros((9 * CH, CH), BF16)
    wd[4 * CH:5 * CH, CH:] = wperc_ref[...]
    for tap in range(9):
        wb[tap * CH:(tap + 1) * CH] = wdv[(8 - tap) * CH:(9 - tap) * CH].T
    wb[9 * CH:] = wperc_ref[...].T
    loads[5].wait()
    loads[6].wait()

    arrived(0)
    widen_x(-1)
    widen_x(ROWS)
    pre_rows((0, 3))
    disc_rows((1, 2))

    arrived(1)
    widen_x(-2)
    widen_x(ROWS + 1)
    pre_rows((-1, ROWS))
    disc_rows((0, 3))
    back_rows((1, 2))
    weight_rows((1, 2), True)

    arrived(2)
    for side, row in ((0, -2), (1, ROWS + 1)):
        for t in range(FRAMES):
            widen(r3, t, row + 2, rhalo[side, t].astype(F32))
    disc_rows((-1, ROWS))
    back_rows((0, 3))
    weight_rows((0, 3), False)

    def remote(src, dst, send, recv, who):
        cp = pltpu.make_async_remote_copy(
            src_ref=src, dst_ref=dst, send_sem=send, recv_sem=recv,
            device_id=who, device_id_type=MESH,
        )
        cp.start()
        return cp

    mine, theirs = core * HALF, (1 - core) * HALF
    spot = px * NY + py
    swap, scatter, spread, gather, forward = [], [], [], [], []
    for g in range(PARTS):
        span = pl.ds(g * PART, PART)
        swap.append(remote(
            buf.at[pl.ds(pl.multiple_of(theirs + g * PART, 8), PART)], cin.at[span],
            csend.at[g], crecv.at[g], other,
        ))

    def piece(g, q):
        return pl.ds(pl.multiple_of(g * PART + q * PIECE, 8), PIECE)

    def whole(g, q):
        return pl.ds(pl.multiple_of(mine + g * PART + q * PIECE, 8), PIECE)

    def chip_sum(g, q):
        return buf[whole(g, q)] + cin[piece(g, q)]

    for g in range(PARTS):
        swap[g].wait_recv()
        for d in PLANE:
            q = lax.rem(px + d // NY, NX) * NY + lax.rem(py + d % NY, NY)
            red[piece(g, q)] = chip_sum(g, q)
            scatter.append(remote(
                red.at[piece(g, q)], r1.at[g, spot], s1.at[g, d], v1.at[g, d], plane(d)
            ))
        r1[g, spot] = chip_sum(g, spot)
    for g in range(PARTS):
        for cp in scatter[g * len(PLANE):(g + 1) * len(PLANE)]:
            cp.wait_recv()
        total = r1[g, 0]
        for n in range(1, NX * NY):
            total = total + r1[g, n]
        r2[g, pz] = total
        for d in LINE:
            spread.append(remote(
                r2.at[g, pz], r2.at[g, pz], s2.at[g, d], v2.at[g, d], line(d)
            ))
    for g in range(PARTS):
        for cp in spread[g * len(LINE):(g + 1) * len(LINE)]:
            cp.wait_recv()
        total = r2[g, 0]
        for n in range(1, NZ):
            total = total + r2[g, n]
        own = whole(g, spot)
        out_ref[own] = total
        for d in PLANE:
            gather.append(remote(
                out_ref.at[own], out_ref.at[own], s3.at[g, d], v3.at[g, d], plane(d)
            ))
        forward.append(remote(out_ref.at[own], out_ref.at[own], s4.at[g, 0], v4.at[g, 0], other))
    for g in range(PARTS):
        for n, d in enumerate(PLANE):
            q = lax.rem(px + NX - d // NY, NX) * NY + lax.rem(py + NY - d % NY, NY)
            gather[g * len(PLANE) + n].wait_recv()
            rows = whole(g, q)
            forward.append(remote(
                out_ref.at[rows], out_ref.at[rows], s4.at[g, d], v4.at[g, d], other
            ))
    for cp in forward:
        cp.wait_recv()

    @pl.when(has_up)
    def _():
        for n in (0, 2, 4):
            halos[n].wait_send()

    @pl.when(has_down)
    def _():
        for n in (1, 3, 5):
            halos[n].wait_send()

    for cp in swap + scatter + spread + gather + forward:
        cp.wait_send()


def per_device(latent, target, w_dec, w_disc, w_head, w_perc):
    hbm = pl.BlockSpec(memory_space=pltpu.HBM)
    vmem = pl.BlockSpec(memory_space=pltpu.VMEM)
    dma = pltpu.SemaphoreType.DMA
    plane, line = NX * NY, NZ
    total = pl.pallas_call(
        kernel,
        out_shape=jax.ShapeDtypeStruct((TAPS * CH, CH), F32),
        in_specs=[hbm] * 6,
        out_specs=vmem,
        scratch_shapes=[
            pltpu.VMEM((FRAMES, ROWS + 4, COLS, CH), BF16),
            pltpu.VMEM((FRAMES, ROWS + 4, COLS, 3 * CH), BF16),
            pltpu.VMEM((FRAMES, ROWS + 2, CH, COLS), BF16),
            pltpu.VMEM((FRAMES, ROWS, COLS, CH), BF16),
            pltpu.VMEM((9 * CH, 2 * CH), BF16),
            pltpu.VMEM((9 * CH, 2 * CH), BF16),
            pltpu.VMEM((10 * CH, CH), BF16),
            pltpu.VMEM((9 * CH, CH), BF16),
            pltpu.VMEM((1, CH), F32),
            pltpu.VMEM((CH, CH), BF16),
            pltpu.VMEM((2, FRAMES, COLS, CH), BF16),
            pltpu.VMEM((2, FRAMES, COLS, CH), BF16),
            pltpu.VMEM((FRAMES, ROWS + 4, COLS, 3 * CH), BF16),
            pltpu.VMEM((FRAMES, ROWS + 2, COLS, 3 * CH), BF16),
            pltpu.VMEM((FRAMES, ROWS, COLS, CH), BF16),
            pltpu.VMEM((FRAMES, ROWS, COLS, CH), F32),
            pltpu.VMEM((FRAMES, ROWS, COLS, 3 * CH), BF16),
            pltpu.VMEM((TAPS * CH, CH), F32),
            pltpu.VMEM((HALF, CH), F32),
            pltpu.VMEM((HALF, CH), F32),
            pltpu.VMEM((PARTS, plane, PIECE, CH), F32),
            pltpu.VMEM((PARTS, line, PIECE, CH), F32),
            dma((7,)), dma((6,)), dma((6,)), dma((PARTS,)), dma((PARTS,)),
            dma((PARTS, plane)), dma((PARTS, plane)), dma((PARTS, line)), dma((PARTS, line)),
            dma((PARTS, plane)), dma((PARTS, plane)), dma((PARTS, plane)), dma((PARTS, plane)),
        ],
        compiler_params=pltpu.CompilerParams(
            collective_id=0, has_side_effects=True, vmem_limit_bytes=48 << 20
        ),
        name="tokenizer_step",
    )(
        *(pltpu.with_memory_space_constraint(x, pltpu.HBM) for x in (
            latent[0], target[0], w_dec.reshape(2, 9 * CH, CH), w_disc.reshape(9 * CH, CH),
            w_head.reshape(1, CH), w_perc,
        ))
    )
    pixels = lax.axis_size("dp") * FRAMES * ROWS * lax.axis_size("sect") * COLS
    total = total / jnp.sqrt(jnp.float32(pixels))
    return total.reshape(2, 3, 3, CH, CH)


def solution(mesh):
    in_specs = (
        P("dp", None, "sect", None, None),
        P("dp", None, "sect", None, None),
        P(),
        P(),
        P(),
        P(),
    )
    return jax.shard_map(
        per_device, mesh=mesh, in_specs=in_specs, out_specs=P(), check_vma=False
    )
```

```python
import functools

import jax
import jax.numpy as jnp
from jax import lax
from jax.experimental import pallas as pl
from jax.experimental.pallas import tpu as pltpu
from jax.sharding import PartitionSpec as P

MESH = pl.DeviceIdType.MESH
F32 = jnp.float32
BF16 = jnp.bfloat16
FRAMES, ROWS, COLS, CH = 2, 4, 256, 128
NX, NY, NZ = 4, 4, 8
TAPS = 18
HALF = TAPS * CH // 2
PARTS = 3
PART = HALF // PARTS
PIECE = PART // (NX * NY)
PLANE = sorted(range(1, NX * NY), key=lambda d: -min(d // NY, NX - d // NY) - min(d % NY, NY - d % NY))
LINE = sorted(range(1, NZ), key=lambda d: -min(d, NZ - d))


def slope(value):
    sig = jax.nn.sigmoid(value)
    return sig * (1.0 + value * (1.0 - sig))


def shifted(tile):
    at = lax.broadcasted_iota(jnp.int32, tile.shape, 0)
    before = jnp.where(at == 0, 0.0, pltpu.roll(tile, 1, 0))
    after = jnp.where(at == COLS - 1, 0.0, pltpu.roll(tile, COLS - 1, 0))
    return before.astype(BF16), tile.astype(BF16), after.astype(BF16)


def dot(a, b):
    return jnp.dot(a, b, preferred_element_type=F32)


def kernel(
    lat_hbm, tgt_hbm, wdec_hbm, wdisc_hbm, whead_hbm, wperc_hbm,
    out_ref,
    xs, x3, xt, tgt, wa, wd, wb, wdv, whead_ref, wperc_ref, rec, rhalo, r3, g3, gf, slp, p3,
    buf, cin, red, r1, r2,
    lsem, hsend, hrecv, sent, crecv, v1, v2, v3, v4,
):
    dp, sect = lax.axis_index("dp"), lax.axis_index("sect")
    core, px = lax.rem(dp, 2), lax.rem(dp // 2, NX)
    py, pz = sect // 2, (dp // 8) * 2 + lax.rem(sect, 2)

    def at(x, y, z, c):
        return ((z // 2) * 8 + x * 2 + c, y * 2 + lax.rem(z, 2))

    other = at(px, py, pz, 1 - core)

    def plane(d):
        return at(lax.rem(px + d // NY, NX), lax.rem(py + d % NY, NY), pz, core)

    def line(d):
        return at(px, py, lax.rem(pz + d, NZ), core)

    up, down = (dp, sect - 1), (dp, sect + 1)
    has_up, has_down = sect > 0, sect < 2 * NY - 1

    bar = pltpu.get_barrier_semaphore()

    def greet(who):
        pl.semaphore_signal(bar, inc=1, device_id=who, device_id_type=MESH)

    @pl.when(has_up)
    def _():
        greet(up)

    @pl.when(has_down)
    def _():
        greet(down)

    greet(other)
    for d in range(1, NX * NY):
        greet(plane(d))
    for d in range(1, NZ):
        greet(line(d))

    loads = [
        pltpu.make_async_copy(lat_hbm, xs.at[:, pl.ds(2, ROWS)], lsem.at[0]),
        pltpu.make_async_copy(wdec_hbm.at[1], wa.at[:, pl.ds(0, CH)], lsem.at[1]),
        pltpu.make_async_copy(wdec_hbm.at[0], wa.at[:, pl.ds(CH, CH)], lsem.at[2]),
        pltpu.make_async_copy(wdisc_hbm, wdv, lsem.at[3]),
        pltpu.make_async_copy(wperc_hbm, wperc_ref, lsem.at[4]),
        pltpu.make_async_copy(whead_hbm, whead_ref, lsem.at[5]),
        pltpu.make_async_copy(tgt_hbm, tgt, lsem.at[6]),
    ]
    for cp in loads:
        cp.start()

    zrow = jnp.zeros((FRAMES, COLS, CH), BF16)

    @pl.when(jnp.logical_not(has_up))
    def _():
        xs[:, 0] = zrow
        xs[:, 1] = zrow
        rhalo[0] = zrow

    @pl.when(jnp.logical_not(has_down))
    def _():
        xs[:, 6] = zrow
        xs[:, 7] = zrow
        rhalo[1] = zrow

    def widen(dst, t, idx, tile):
        for j, piece in enumerate(shifted(tile)):
            dst[t, idx, :, j * CH:(j + 1) * CH] = piece

    def widen_x(row):
        for t in range(FRAMES):
            tile = xs[t, row + 2]
            widen(x3, t, row + 2, tile.astype(F32))
            if -1 <= row <= ROWS:
                xt[t, row + 1] = tile.T

    def around(src, t, idx):
        return jnp.concatenate([src[t, idx - 1], src[t, idx], src[t, idx + 1]], axis=1)

    def pre_rows(rows):
        first = dot(jnp.concatenate([around(x3, 0, r + 2) for r in rows], axis=0), wa[...])
        second = dot(jnp.concatenate([around(x3, 1, r + 2) for r in rows], axis=0), wa[:, :CH])
        for n, r in enumerate(rows):
            span = slice(n * COLS, (n + 1) * COLS)
            for t in range(FRAMES):
                pre = first[span, :CH] if t == 0 else first[span, CH:] + second[span]
                sig = jax.nn.sigmoid(pre)
                value = pre * sig
                if r < 0:
                    value = jnp.where(has_up, value, 0.0)
                elif r >= ROWS:
                    value = jnp.where(has_down, value, 0.0)
                else:
                    slp[t, r] = sig * (1.0 + pre * (1.0 - sig))
                widen(r3, t, r + 2, value)
                if r in (1, 2):
                    rec[2 - r, t] = value.astype(BF16)

    def disc_rows(rows):
        own = 0 <= rows[0] < ROWS
        lhs = jnp.concatenate([around(r3, t, r + 2) for r in rows for t in range(FRAMES)], axis=0)
        res = dot(lhs, wd[...] if own else wd[:, :CH])
        for n, (r, t) in enumerate([(r, t) for r in rows for t in range(FRAMES)]):
            span = slice(n * COLS, (n + 1) * COLS)
            grad = -whead_ref[...] * slope(res[span, :CH])
            if r < 0:
                grad = jnp.where(has_up, grad, 0.0)
            elif r >= ROWS:
                grad = jnp.where(has_down, grad, 0.0)
            else:
                gf[t, r] = (res[span, CH:] - tgt[t, r].astype(F32)).astype(BF16)
            widen(g3, t, r + 1, grad)

    def back_rows(rows):
        pairs = [(r, t) for r in rows for t in range(FRAMES)]
        lhs = jnp.concatenate(
            [jnp.concatenate([around(g3, t, r + 1), gf[t, r]], axis=1) for r, t in pairs], axis=0
        )
        res = dot(lhs, wb[...])
        for n, (r, t) in enumerate(pairs):
            grad = res[n * COLS:(n + 1) * COLS] * slp[t, r]
            for j, piece in enumerate(shifted(grad)):
                p3[t, r, :, (2 - j) * CH:(3 - j) * CH] = piece

    def weight_rows(rows, first):
        def left(t, r):
            return xt[t, r:r + 3].reshape(3 * CH, COLS)

        lhs0 = jnp.concatenate([left(0, r) for r in rows], axis=1)
        rhs1 = jnp.concatenate([p3[1, r] for r in rows], axis=0)
        k0 = dot(lhs0, rhs1)
        lhs1 = jnp.concatenate([lhs0] + [left(1, r) for r in rows], axis=1)
        rhs = jnp.concatenate([p3[0, r] for r in rows] + [rhs1], axis=0)
        k1 = dot(lhs1, rhs)
        for k, res in enumerate((k0, k1)):
            for i in range(3):
                for j in range(3):
                    piece = res[i * CH:(i + 1) * CH, j * CH:(j + 1) * CH]
                    span = pl.ds(((k * 3 + i) * 3 + j) * CH, CH)
                    if first:
                        buf[span] = piece
                    else:
                        buf[span] += piece

    loads[0].wait()
    for row in range(ROWS):
        widen_x(row)
    loads[1].wait()
    loads[2].wait()
    pre_rows((1, 2))

    pl.semaphore_wait(bar, NX * NY - 1 + NZ - 1 + 1 + has_up.astype(jnp.int32) + has_down.astype(jnp.int32))

    def halo(n, src, dst, who):
        return pltpu.make_async_remote_copy(
            src_ref=src, dst_ref=dst, send_sem=hsend.at[n], recv_sem=hrecv.at[n],
            device_id=who, device_id_type=MESH,
        )

    halos = [
        halo(0, lat_hbm.at[:, 0], xs.at[:, 6], up),
        halo(1, lat_hbm.at[:, 3], xs.at[:, 1], down),
        halo(2, lat_hbm.at[:, 1], xs.at[:, 7], up),
        halo(3, lat_hbm.at[:, 2], xs.at[:, 0], down),
        halo(4, rec.at[1], rhalo.at[1], up),
        halo(5, rec.at[0], rhalo.at[0], down),
    ]

    @pl.when(has_up)
    def _():
        for n in (0,):
            halos[n].start()

    @pl.when(has_down)
    def _():
        for n in (1,):
            halos[n].start()

    @pl.when(has_up)
    def _():
        for n in (2,):
            halos[n].start()

    @pl.when(has_down)
    def _():
        for n in (3,):
            halos[n].start()

    @pl.when(has_up)
    def _():
        for n in (4,):
            halos[n].start()

    @pl.when(has_down)
    def _():
        for n in (5,):
            halos[n].start()


    def arrived(pair):
        @pl.when(has_down)
        def _():
            halos[2 * pair].wait_recv()

        @pl.when(has_up)
        def _():
            halos[2 * pair + 1].wait_recv()

    loads[3].wait()
    loads[4].wait()
    wd[:, :CH] = wdv[...]
    wd[:, CH:] = jnp.zeros((9 * CH, CH), BF16)
    wd[4 * CH:5 * CH, CH:] = wperc_ref[...]
    for tap in range(9):
        wb[tap * CH:(tap + 1) * CH] = wdv[(8 - tap) * CH:(9 - tap) * CH].T
    wb[9 * CH:] = wperc_ref[...].T
    loads[5].wait()
    loads[6].wait()

    arrived(0)
    widen_x(-1)
    widen_x(ROWS)
    pre_rows((0, 3))
    disc_rows((1, 2))

    arrived(1)
    widen_x(-2)
    widen_x(ROWS + 1)
    pre_rows((-1, ROWS))
    disc_rows((0, 3))
    back_rows((1, 2))
    weight_rows((1, 2), True)

    arrived(2)
    for side, row in ((0, -2), (1, ROWS + 1)):
        for t in range(FRAMES):
            widen(r3, t, row + 2, rhalo[side, t].astype(F32))
    disc_rows((-1, ROWS))
    back_rows((0, 3))
    weight_rows((0, 3), False)

    def remote(src, dst, send, recv, who):
        pltpu.make_async_remote_copy(
            src_ref=src, dst_ref=dst, send_sem=send, recv_sem=recv,
            device_id=who, device_id_type=MESH,
        ).start()

    def settle(like, sem):
        pltpu.make_async_copy(like, like, sem).wait()

    mine, theirs = core * HALF, (1 - core) * HALF
    spot = px * NY + py
    for g in range(PARTS):
        remote(
            buf.at[pl.ds(pl.multiple_of(theirs + g * PART, 8), PART)],
            cin.at[pl.ds(g * PART, PART)], sent.at[0], crecv.at[g], other,
        )

    def piece(g, q):
        return pl.ds(pl.multiple_of(g * PART + q * PIECE, 8), PIECE)

    def whole(g, q):
        return pl.ds(pl.multiple_of(mine + g * PART + q * PIECE, 8), PIECE)

    for g in range(PARTS):
        part = pl.ds(g * PART, PART)
        settle(cin.at[part], crecv.at[g])
        red[part] = buf[pl.ds(pl.multiple_of(mine + g * PART, 8), PART)] + cin[part]
        for d in PLANE:
            q = lax.rem(px + d // NY, NX) * NY + lax.rem(py + d % NY, NY)
            remote(red.at[piece(g, q)], r1.at[g, spot], sent.at[1], v1.at[g], plane(d))
        r1[g, spot] = red[piece(g, spot)]
    for g in range(PARTS):
        settle(r1.at[g, pl.ds(0, len(PLANE))], v1.at[g])
        total = r1[g, 0]
        for n in range(1, NX * NY):
            total = total + r1[g, n]
        r2[g, pz] = total
        for d in LINE:
            remote(r2.at[g, pz], r2.at[g, pz], sent.at[2], v2.at[g], line(d))
    for g in range(PARTS):
        settle(r2.at[g, pl.ds(0, len(LINE))], v2.at[g])
        total = r2[g, 0]
        for n in range(1, NZ):
            total = total + r2[g, n]
        own = whole(g, spot)
        out_ref[own] = total
        for d in PLANE:
            remote(out_ref.at[own], out_ref.at[own], sent.at[3], v3.at[g], plane(d))
    for g in range(PARTS):
        settle(r1.at[g, pl.ds(0, len(PLANE))], v3.at[g])
        rows = pl.ds(pl.multiple_of(mine + g * PART, 8), PART)
        remote(out_ref.at[rows], out_ref.at[rows], sent.at[4], v4, other)
    settle(cin, v4)

    @pl.when(has_up)
    def _():
        for n in (0, 2, 4):
            halos[n].wait_send()

    @pl.when(has_down)
    def _():
        for n in (1, 3, 5):
            halos[n].wait_send()

    settle(cin, sent.at[0])
    settle(red.at[pl.ds(0, PARTS * len(PLANE) * PIECE)], sent.at[1])
    settle(red.at[pl.ds(0, PARTS * len(LINE) * PIECE)], sent.at[2])
    settle(red.at[pl.ds(0, PARTS * len(PLANE) * PIECE)], sent.at[3])
    settle(cin, sent.at[4])


def per_device(latent, target, w_dec, w_disc, w_head, w_perc):
    hbm = pl.BlockSpec(memory_space=pltpu.HBM)
    vmem = pl.BlockSpec(memory_space=pltpu.VMEM)
    dma = pltpu.SemaphoreType.DMA
    plane, line = NX * NY, NZ
    total = pl.pallas_call(
        kernel,
        out_shape=jax.ShapeDtypeStruct((TAPS * CH, CH), F32),
        in_specs=[hbm] * 6,
        out_specs=vmem,
        scratch_shapes=[
            pltpu.VMEM((FRAMES, ROWS + 4, COLS, CH), BF16),
            pltpu.VMEM((FRAMES, ROWS + 4, COLS, 3 * CH), BF16),
            pltpu.VMEM((FRAMES, ROWS + 2, CH, COLS), BF16),
            pltpu.VMEM((FRAMES, ROWS, COLS, CH), BF16),
            pltpu.VMEM((9 * CH, 2 * CH), BF16),
            pltpu.VMEM((9 * CH, 2 * CH), BF16),
            pltpu.VMEM((10 * CH, CH), BF16),
            pltpu.VMEM((9 * CH, CH), BF16),
            pltpu.VMEM((1, CH), F32),
            pltpu.VMEM((CH, CH), BF16),
            pltpu.VMEM((2, FRAMES, COLS, CH), BF16),
            pltpu.VMEM((2, FRAMES, COLS, CH), BF16),
            pltpu.VMEM((FRAMES, ROWS + 4, COLS, 3 * CH), BF16),
            pltpu.VMEM((FRAMES, ROWS + 2, COLS, 3 * CH), BF16),
            pltpu.VMEM((FRAMES, ROWS, COLS, CH), BF16),
            pltpu.VMEM((FRAMES, ROWS, COLS, CH), F32),
            pltpu.VMEM((FRAMES, ROWS, COLS, 3 * CH), BF16),
            pltpu.VMEM((TAPS * CH, CH), F32),
            pltpu.VMEM((HALF, CH), F32),
            pltpu.VMEM((HALF, CH), F32),
            pltpu.VMEM((PARTS, plane, PIECE, CH), F32),
            pltpu.VMEM((PARTS, line, PIECE, CH), F32),
            dma((7,)), dma((6,)), dma((6,)), dma((5,)), dma((PARTS,)),
            dma((PARTS,)), dma((PARTS,)), dma((PARTS,)), dma,
        ],
        compiler_params=pltpu.CompilerParams(
            collective_id=0, has_side_effects=True, vmem_limit_bytes=48 << 20
        ),
        name="tokenizer_step",
    )(
        *(pltpu.with_memory_space_constraint(x, pltpu.HBM) for x in (
            latent[0], target[0], w_dec.reshape(2, 9 * CH, CH), w_disc.reshape(9 * CH, CH),
            w_head.reshape(1, CH), w_perc,
        ))
    )
    pixels = lax.axis_size("dp") * FRAMES * ROWS * lax.axis_size("sect") * COLS
    total = total / jnp.sqrt(jnp.float32(pixels))
    return total.reshape(2, 3, 3, CH, CH)


def solution(mesh):
    in_specs = (
        P("dp", None, "sect", None, None),
        P("dp", None, "sect", None, None),
        P(),
        P(),
        P(),
        P(),
    )
    return jax.shard_map(
        per_device, mesh=mesh, in_specs=in_specs, out_specs=P(), check_vma=False
    )
```

```python
import functools

import jax
import jax.numpy as jnp
from jax import lax
from jax.experimental import pallas as pl
from jax.experimental.pallas import tpu as pltpu
from jax.sharding import PartitionSpec as P

MESH = pl.DeviceIdType.MESH
F32 = jnp.float32
BF16 = jnp.bfloat16
FRAMES, ROWS, COLS, CH = 2, 4, 256, 128
NX, NY, NZ = 4, 4, 8
TAPS = 18
HALF = TAPS * CH // 2
PARTS = 3
PART = HALF // PARTS
PIECE = PART // (NX * NY)
PLANE = sorted(range(1, NX * NY), key=lambda d: -min(d // NY, NX - d // NY) - min(d % NY, NY - d % NY))
LINE = sorted(range(1, NZ), key=lambda d: -min(d, NZ - d))


def slope(value):
    sig = jax.nn.sigmoid(value)
    return sig * (1.0 + value * (1.0 - sig))


def shifted(tile):
    at = lax.broadcasted_iota(jnp.int32, tile.shape, 0)
    before = jnp.where(at == 0, 0.0, pltpu.roll(tile, 1, 0))
    after = jnp.where(at == COLS - 1, 0.0, pltpu.roll(tile, COLS - 1, 0))
    return before.astype(BF16), tile.astype(BF16), after.astype(BF16)


def dot(a, b):
    return jnp.dot(a, b, preferred_element_type=F32)


def kernel(
    lat_hbm, tgt_hbm, wdec_hbm, wdisc_hbm, whead_hbm, wperc_hbm,
    out_ref,
    xs, x3, xt, tgt, wa, wx, wd, wb, wp, wq, wdv, whead_ref, wperc_ref, rec, rhalo, r3, g3, feat, slp, p3,
    buf, cin, red, r1, r2,
    lsem, hsend, hrecv, near, tsem, sent, crecv, v1, v2, v3, v4,
):
    dp, sect = lax.axis_index("dp"), lax.axis_index("sect")
    core, px = lax.rem(dp, 2), lax.rem(dp // 2, NX)
    py, pz = sect // 2, (dp // 8) * 2 + lax.rem(sect, 2)

    def at(x, y, z, c):
        return ((z // 2) * 8 + x * 2 + c, y * 2 + lax.rem(z, 2))

    other = at(px, py, pz, 1 - core)

    def plane(d):
        return at(lax.rem(px + d // NY, NX), lax.rem(py + d % NY, NY), pz, core)

    def line(d):
        return at(px, py, lax.rem(pz + d, NZ), core)

    low = lax.rem(pz, 2)
    home = low == core
    block = 2 * py + core
    has_up, has_down = block > 0, block < 2 * NY - 1
    partner = at(px, py, pz + 1 - 2 * low, 1 - core)
    up = at(px, py - (1 - core), pz, 1 - core)
    down = at(px, py + core, pz, 1 - core)

    bar = pltpu.get_barrier_semaphore()

    def greet(who):
        pl.semaphore_signal(bar, inc=1, device_id=who, device_id_type=MESH)

    @pl.when(has_up)
    def _():
        greet(up)

    @pl.when(has_down)
    def _():
        greet(down)

    greet(partner)
    greet(other)
    for d in range(1, NX * NY):
        greet(plane(d))
    for d in range(1, NZ):
        greet(line(d))

    loads = [
        pltpu.make_async_copy(wdec_hbm.at[1], wa.at[:, pl.ds(0, CH)], lsem.at[0]),
        pltpu.make_async_copy(wdec_hbm.at[0], wa.at[:, pl.ds(CH, CH)], lsem.at[1]),
        pltpu.make_async_copy(wdisc_hbm, wdv, lsem.at[2]),
        pltpu.make_async_copy(wperc_hbm, wperc_ref, lsem.at[3]),
        pltpu.make_async_copy(whead_hbm, whead_ref, lsem.at[4]),
    ]
    for cp in loads:
        cp.start()

    zrow = jnp.zeros((FRAMES, COLS, CH), BF16)

    @pl.when(jnp.logical_not(has_up))
    def _():
        xs[:, 0] = zrow
        xs[:, 1] = zrow
        rhalo[0] = zrow

    @pl.when(jnp.logical_not(has_down))
    def _():
        xs[:, 6] = zrow
        xs[:, 7] = zrow
        rhalo[1] = zrow

    def widen(dst, t, idx, tile):
        for j, piece in enumerate(shifted(tile)):
            dst[t, idx, :, j * CH:(j + 1) * CH] = piece

    def widen_x(row):
        for t in range(FRAMES):
            tile = xs[t, row + 2]
            widen(x3, t, row + 2, tile.astype(F32))
            if -1 <= row <= ROWS:
                xt[t, row + 1] = tile.T

    def around(src, t, idx):
        return jnp.concatenate([src[t, idx - 1], src[t, idx], src[t, idx + 1]], axis=1)

    def four(src, t, idx):
        return jnp.concatenate([src[t, idx + q] for q in range(4)], axis=1)

    def pre_rows(r):
        first = dot(jnp.concatenate([around(x3, 0, r + 2 + n) for n in range(2)], axis=0), wa[...])
        second = dot(four(x3, 1, r + 1), wx[...])
        for n in range(2):
            row, span = r + n, slice(n * COLS, (n + 1) * COLS)
            for t in range(FRAMES):
                pre = first[span, :CH] if t == 0 else first[span, CH:] + second[:, n * CH:(n + 1) * CH]
                sig = jax.nn.sigmoid(pre)
                value = pre * sig
                if row < 0:
                    value = jnp.where(has_up, value, 0.0)
                elif row >= ROWS:
                    value = jnp.where(has_down, value, 0.0)
                else:
                    slp[t, row] = sig * (1.0 + pre * (1.0 - sig))
                widen(r3, t, row + 2, value)
                if row in (1, 2):
                    rec[2 - row, t] = value.astype(BF16)

    def disc_rows(r):
        res = dot(jnp.concatenate([four(r3, t, r + 1) for t in range(FRAMES)], axis=0), wd[...])
        for n in range(2):
            row = r + n
            for t in range(FRAMES):
                grad = -whead_ref[...] * slope(res[t * COLS:(t + 1) * COLS, n * CH:(n + 1) * CH])
                if row < 0:
                    grad = jnp.where(has_up, grad, 0.0)
                elif row >= ROWS:
                    grad = jnp.where(has_down, grad, 0.0)
                widen(g3, t, row + 1, grad)

    def feat_rows():
        lhs = [
            jnp.concatenate([r3[t, r + 2 + n, :, CH:2 * CH] for n in range(2)], axis=1)
            for r in (0, 2) for t in range(FRAMES)
        ]
        feat[...] = dot(jnp.concatenate(lhs, axis=0), wp[...])

    def back_rows(r):
        return dot(jnp.concatenate([four(g3, t, r) for t in range(FRAMES)], axis=0), wb[...])

    def grad_rows(r, back):
        miss = []
        for t in range(FRAMES):
            at_row = (r + t) * COLS
            goal = jnp.concatenate([tgt[t, r + n].astype(F32) for n in range(2)], axis=1)
            miss.append((feat[at_row:at_row + COLS] - goal).astype(BF16))
        res = back + dot(jnp.concatenate(miss, axis=0), wq[...])
        for n in range(2):
            for t in range(FRAMES):
                grad = res[t * COLS:(t + 1) * COLS, n * CH:(n + 1) * CH] * slp[t, r + n]
                for j, piece in enumerate(shifted(grad)):
                    lane = (t * 3 + 2 - j) * CH
                    p3[(r + n) * COLS:(r + n + 1) * COLS, lane:lane + CH] = piece

    def weight_rows():
        def left(t):
            return jnp.concatenate([xt[t, r:r + 3].reshape(3 * CH, COLS) for r in range(ROWS)], axis=1)

        both = dot(left(0), p3[...])
        late = dot(left(1), p3[:, 3 * CH:])
        for k in range(2):
            for i in range(3):
                for j in range(3):
                    rows, lanes = slice(i * CH, (i + 1) * CH), slice(j * CH, (j + 1) * CH)
                    span = pl.ds(((k * 3 + i) * 3 + j) * CH, CH)
                    if k:
                        buf[span] = both[rows, lanes] + late[rows, lanes]
                    else:
                        buf[span] = both[rows, (3 + j) * CH:(4 + j) * CH]

    def remote(src, dst, send, recv, who):
        cp = pltpu.make_async_remote_copy(
            src_ref=src, dst_ref=dst, send_sem=send, recv_sem=recv,
            device_id=who, device_id_type=MESH,
        )
        cp.start()

    def settle(like, sem):
        pltpu.make_async_copy(like, like, sem).wait()

    ROW, FOUR = xs.at[:, 0], xs.at[:, pl.ds(0, ROWS)]

    @pl.when(home)
    def _():
        for row in range(ROWS):
            pltpu.make_async_copy(lat_hbm.at[:, row], xs.at[:, row + 2], hrecv.at[row]).start()
        pltpu.make_async_copy(tgt_hbm, tgt, tsem).start()

    pl.semaphore_wait(bar, NX * NY - 1 + NZ - 1 + 2 + has_up.astype(jnp.int32) + has_down.astype(jnp.int32))

    def order(c, k):
        return k + c * (ROWS - 1 - 2 * k)

    @pl.when(jnp.logical_not(home))
    def _():
        for k in range(ROWS):
            row = order(1 - core, k)
            remote(lat_hbm.at[:, row], xs.at[:, row + 2], hsend.at[0], hrecv.at[row], partner)
        remote(tgt_hbm, tgt, hsend.at[1], tsem, partner)

    for n in (2, 3, 4):
        loads[n].wait()

    def band(dst, tap):
        dst[...] = jnp.zeros_like(dst)
        for n in range(2):
            for i in range(3):
                for j in range(3):
                    row = ((i + n) * 3 + j) * CH
                    dst[row:row + CH, n * CH:(n + 1) * CH] = tap(i * 3 + j)

    band(wd, lambda k: wdv[k * CH:(k + 1) * CH])
    band(wb, lambda k: wdv[(8 - k) * CH:(9 - k) * CH].T)
    loads[0].wait()
    band(wx, lambda k: wa[k * CH:(k + 1) * CH, :CH])
    loads[1].wait()
    wp[...] = jnp.zeros_like(wp)
    wq[...] = jnp.zeros_like(wq)
    for n in range(2):
        span = slice(n * CH, (n + 1) * CH)
        wp[span, span] = wperc_ref[...]
        wq[span, span] = wperc_ref[...].T

    def pass_on(row):
        settle(ROW, hrecv.at[row])
        if row <= 1:
            @pl.when(has_up)
            def _():
                remote(xs.at[:, row + 2], xs.at[:, row + 6], hsend.at[2], near.at[2 + row], up)
        else:
            @pl.when(has_down)
            def _():
                remote(xs.at[:, row + 2], xs.at[:, row - 2], hsend.at[3], near.at[3 - row], down)
        widen_x(row)

    @pl.when(core == 0)
    def _():
        for row in range(ROWS):
            pass_on(row)

    @pl.when(core == 1)
    def _():
        for row in reversed(range(ROWS)):
            pass_on(row)

    pre_rows(1)

    @pl.when(has_up)
    def _():
        remote(rec.at[1], rhalo.at[1], hsend.at[2], near.at[5], up)

    @pl.when(has_down)
    def _():
        remote(rec.at[0], rhalo.at[0], hsend.at[3], near.at[4], down)

    def arrived(step):
        @pl.when(has_up)
        def _():
            settle(ROW, near.at[(0, 1, 4)[step]])

        @pl.when(has_down)
        def _():
            settle(ROW, near.at[(2, 3, 5)[step]])

    arrived(0)
    widen_x(-1)
    widen_x(ROWS)
    arrived(1)
    widen_x(-2)
    widen_x(ROWS + 1)
    pre_rows(-1)
    pre_rows(ROWS - 1)
    feat_rows()
    disc_rows(1)

    arrived(2)
    for side, row in ((0, -2), (1, ROWS + 1)):
        for t in range(FRAMES):
            widen(r3, t, row + 2, rhalo[side, t].astype(F32))
    disc_rows(-1)
    disc_rows(ROWS - 1)
    back = [back_rows(r) for r in (0, 2)]
    settle(FOUR, tsem)
    for n in range(2):
        grad_rows(2 * n, back[n])
    weight_rows()

    mine, theirs = core * HALF, (1 - core) * HALF
    spot = px * NY + py
    for g in range(PARTS):
        remote(
            buf.at[pl.ds(pl.multiple_of(theirs + g * PART, 8), PART)],
            cin.at[pl.ds(g * PART, PART)], sent.at[0], crecv.at[g], other,
        )

    def piece(g, q):
        return pl.ds(pl.multiple_of(g * PART + q * PIECE, 8), PIECE)

    def whole(g, q):
        return pl.ds(pl.multiple_of(mine + g * PART + q * PIECE, 8), PIECE)

    for g in range(PARTS):
        part = pl.ds(g * PART, PART)
        settle(cin.at[part], crecv.at[g])
        red[part] = buf[pl.ds(pl.multiple_of(mine + g * PART, 8), PART)] + cin[part]
        for d in PLANE:
            q = lax.rem(px + d // NY, NX) * NY + lax.rem(py + d % NY, NY)
            remote(red.at[piece(g, q)], r1.at[g, spot], sent.at[1], v1.at[g], plane(d))
        r1[g, spot] = red[piece(g, spot)]
    for g in range(PARTS):
        settle(r1.at[g, pl.ds(0, len(PLANE))], v1.at[g])
        total = r1[g, 0]
        for n in range(1, NX * NY):
            total = total + r1[g, n]
        r2[g, pz] = total
        for d in LINE:
            remote(r2.at[g, pz], r2.at[g, pz], sent.at[2], v2.at[g], line(d))
    for g in range(PARTS):
        settle(r2.at[g, pl.ds(0, len(LINE))], v2.at[g])
        total = r2[g, 0]
        for n in range(1, NZ):
            total = total + r2[g, n]
        own = whole(g, spot)
        out_ref[own] = total
        for d in PLANE:
            remote(out_ref.at[own], out_ref.at[own], sent.at[3], v3.at[g], plane(d))
    for g in range(PARTS):
        settle(r1.at[g, pl.ds(0, len(PLANE))], v3.at[g])
        rows = pl.ds(pl.multiple_of(mine + g * PART, 8), PART)
        remote(out_ref.at[rows], out_ref.at[rows], sent.at[4], v4, other)
    settle(cin, v4)

    @pl.when(jnp.logical_not(home))
    def _():
        settle(FOUR, hsend.at[0])
        settle(FOUR, hsend.at[1])

    @pl.when(has_up)
    def _():
        settle(xs.at[:, pl.ds(0, 3)], hsend.at[2])

    @pl.when(has_down)
    def _():
        settle(xs.at[:, pl.ds(0, 3)], hsend.at[3])

    settle(cin, sent.at[0])
    settle(red.at[pl.ds(0, PARTS * len(PLANE) * PIECE)], sent.at[1])
    settle(red.at[pl.ds(0, PARTS * len(LINE) * PIECE)], sent.at[2])
    settle(red.at[pl.ds(0, PARTS * len(PLANE) * PIECE)], sent.at[3])
    settle(cin, sent.at[4])


def per_device(latent, target, w_dec, w_disc, w_head, w_perc):
    hbm = pl.BlockSpec(memory_space=pltpu.HBM)
    vmem = pl.BlockSpec(memory_space=pltpu.VMEM)
    dma = pltpu.SemaphoreType.DMA
    plane, line = NX * NY, NZ
    total = pl.pallas_call(
        kernel,
        out_shape=jax.ShapeDtypeStruct((TAPS * CH, CH), F32),
        in_specs=[hbm] * 6,
        out_specs=vmem,
        scratch_shapes=[
            pltpu.VMEM((FRAMES, ROWS + 4, COLS, CH), BF16),
            pltpu.VMEM((FRAMES, ROWS + 4, COLS, 3 * CH), BF16),
            pltpu.VMEM((FRAMES, ROWS + 2, CH, COLS), BF16),
            pltpu.VMEM((FRAMES, ROWS, COLS, CH), BF16),
            pltpu.VMEM((9 * CH, 2 * CH), BF16),
            pltpu.VMEM((12 * CH, 2 * CH), BF16),
            pltpu.VMEM((12 * CH, 2 * CH), BF16),
            pltpu.VMEM((12 * CH, 2 * CH), BF16),
            pltpu.VMEM((2 * CH, 2 * CH), BF16),
            pltpu.VMEM((2 * CH, 2 * CH), BF16),
            pltpu.VMEM((9 * CH, CH), BF16),
            pltpu.VMEM((1, CH), F32),
            pltpu.VMEM((CH, CH), BF16),
            pltpu.VMEM((2, FRAMES, COLS, CH), BF16),
            pltpu.VMEM((2, FRAMES, COLS, CH), BF16),
            pltpu.VMEM((FRAMES, ROWS + 4, COLS, 3 * CH), BF16),
            pltpu.VMEM((FRAMES, ROWS + 2, COLS, 3 * CH), BF16),
            pltpu.VMEM((FRAMES * ROWS * COLS // 2, 2 * CH), F32),
            pltpu.VMEM((FRAMES, ROWS, COLS, CH), F32),
            pltpu.VMEM((ROWS * COLS, FRAMES * 3 * CH), BF16),
            pltpu.VMEM((TAPS * CH, CH), F32),
            pltpu.VMEM((HALF, CH), F32),
            pltpu.VMEM((HALF, CH), F32),
            pltpu.VMEM((PARTS, plane, PIECE, CH), F32),
            pltpu.VMEM((PARTS, line, PIECE, CH), F32),
            dma((5,)), dma((4,)), dma((ROWS,)), dma((6,)), dma, dma((5,)), dma((PARTS,)),
            dma((PARTS,)), dma((PARTS,)), dma((PARTS,)), dma,
        ],
        compiler_params=pltpu.CompilerParams(
            collective_id=0, has_side_effects=True, vmem_limit_bytes=48 << 20
        ),
        name="tokenizer_step",
    )(
        *(pltpu.with_memory_space_constraint(x, pltpu.HBM) for x in (
            latent[0], target[0], w_dec.reshape(2, 9 * CH, CH), w_disc.reshape(9 * CH, CH),
            w_head.reshape(1, CH), w_perc,
        ))
    )
    pixels = lax.axis_size("dp") * FRAMES * ROWS * lax.axis_size("sect") * COLS
    total = total / jnp.sqrt(jnp.float32(pixels))
    return total.reshape(2, 3, 3, CH, CH)


def solution(mesh):
    in_specs = (
        P("dp", None, "sect", None, None),
        P("dp", None, "sect", None, None),
        P(),
        P(),
        P(),
        P(),
    )
    return jax.shard_map(
        per_device, mesh=mesh, in_specs=in_specs, out_specs=P(), check_vma=False
    )
```

```python
import functools

import jax
import jax.numpy as jnp
from jax import lax
from jax.experimental import pallas as pl
from jax.experimental.pallas import tpu as pltpu
from jax.sharding import PartitionSpec as P

MESH = pl.DeviceIdType.MESH
F32 = jnp.float32
BF16 = jnp.bfloat16
FRAMES, ROWS, COLS, CH = 2, 4, 256, 128
NX, NY, NZ = 4, 4, 8
TAPS = 18
HALF = TAPS * CH // 2
PARTS = 9
LINED = [0, 3, 6]
PART = HALF // PARTS
PIECE = PART // (NX * NY)
PLANE = sorted(range(1, NX * NY), key=lambda d: -min(d // NY, NX - d // NY) - min(d % NY, NY - d % NY))
LINE = sorted(range(1, NZ), key=lambda d: -min(d, NZ - d))


def slope(value):
    sig = jax.nn.sigmoid(value)
    return sig * (1.0 + value * (1.0 - sig))


def shifted(tile):
    at = lax.broadcasted_iota(jnp.int32, tile.shape, 0)
    before = jnp.where(at == 0, 0.0, pltpu.roll(tile, 1, 0))
    after = jnp.where(at == COLS - 1, 0.0, pltpu.roll(tile, COLS - 1, 0))
    return before.astype(BF16), tile.astype(BF16), after.astype(BF16)


def dot(a, b):
    return jnp.dot(a, b, preferred_element_type=F32)


def kernel(
    lat_hbm, tgt_hbm, wdec_hbm, wdisc_hbm, whead_hbm, wperc_hbm,
    out_ref,
    xs, x3, xt, tgt, wa, wx, wd, wb, wp, wq, wdv, whead_ref, wperc_ref, rec, rhalo, r3, g3, feat, slp, p3,
    buf, cin, red, r1, r2, l1, l2,
    lsem, hsend, hrecv, near, tsem, sent, crecv, v1, v2, v3, v4,
):
    dp, sect = lax.axis_index("dp"), lax.axis_index("sect")
    core, px = lax.rem(dp, 2), lax.rem(dp // 2, NX)
    py, pz = sect // 2, (dp // 8) * 2 + lax.rem(sect, 2)

    def at(x, y, z, c):
        return ((z // 2) * 8 + x * 2 + c, y * 2 + lax.rem(z, 2))

    other = at(px, py, pz, 1 - core)

    def plane(d):
        return at(lax.rem(px + d // NY, NX), lax.rem(py + d % NY, NY), pz, core)

    def line(d):
        return at(px, py, lax.rem(pz + d, NZ), core)

    low = lax.rem(pz, 2)
    home = low == core
    block = 2 * py + core
    has_up, has_down = block > 0, block < 2 * NY - 1
    partner = at(px, py, pz + 1 - 2 * low, 1 - core)
    up = at(px, py - (1 - core), pz, 1 - core)
    down = at(px, py + core, pz, 1 - core)

    bar = pltpu.get_barrier_semaphore()

    def greet(who):
        pl.semaphore_signal(bar, inc=1, device_id=who, device_id_type=MESH)

    @pl.when(has_up)
    def _():
        greet(up)

    @pl.when(has_down)
    def _():
        greet(down)

    greet(partner)
    greet(other)
    for d in range(1, NX * NY):
        greet(plane(d))
    for d in range(1, NZ):
        greet(line(d))

    loads = [
        pltpu.make_async_copy(wdec_hbm.at[1], wa.at[:, pl.ds(0, CH)], lsem.at[0]),
        pltpu.make_async_copy(wdec_hbm.at[0], wa.at[:, pl.ds(CH, CH)], lsem.at[1]),
        pltpu.make_async_copy(wdisc_hbm, wdv, lsem.at[2]),
        pltpu.make_async_copy(wperc_hbm, wperc_ref, lsem.at[3]),
        pltpu.make_async_copy(whead_hbm, whead_ref, lsem.at[4]),
    ]
    for cp in loads:
        cp.start()

    zrow = jnp.zeros((FRAMES, COLS, CH), BF16)

    @pl.when(jnp.logical_not(has_up))
    def _():
        xs[:, 0] = zrow
        xs[:, 1] = zrow
        rhalo[0] = zrow

    @pl.when(jnp.logical_not(has_down))
    def _():
        xs[:, 6] = zrow
        xs[:, 7] = zrow
        rhalo[1] = zrow

    def widen(dst, t, idx, tile):
        for j, piece in enumerate(shifted(tile)):
            dst[t, idx, :, j * CH:(j + 1) * CH] = piece

    def widen_x(row):
        for t in range(FRAMES):
            tile = xs[t, row + 2]
            widen(x3, t, row + 2, tile.astype(F32))
            if -1 <= row <= ROWS:
                xt[t, row + 1] = tile.T

    def around(src, t, idx):
        return jnp.concatenate([src[t, idx - 1], src[t, idx], src[t, idx + 1]], axis=1)

    def four(src, t, idx):
        return jnp.concatenate([src[t, idx + q] for q in range(4)], axis=1)

    def pre_rows(r):
        first = dot(jnp.concatenate([around(x3, 0, r + 2 + n) for n in range(2)], axis=0), wa[...])
        second = dot(four(x3, 1, r + 1), wx[...])
        for n in range(2):
            row, span = r + n, slice(n * COLS, (n + 1) * COLS)
            for t in range(FRAMES):
                pre = first[span, :CH] if t == 0 else first[span, CH:] + second[:, n * CH:(n + 1) * CH]
                sig = jax.nn.sigmoid(pre)
                value = pre * sig
                if row < 0:
                    value = jnp.where(has_up, value, 0.0)
                elif row >= ROWS:
                    value = jnp.where(has_down, value, 0.0)
                else:
                    slp[t, row] = sig * (1.0 + pre * (1.0 - sig))
                widen(r3, t, row + 2, value)
                if row in (1, 2):
                    rec[2 - row, t] = value.astype(BF16)

    def disc_rows(r):
        res = dot(jnp.concatenate([four(r3, t, r + 1) for t in range(FRAMES)], axis=0), wd[...])
        for n in range(2):
            row = r + n
            for t in range(FRAMES):
                grad = -whead_ref[...] * slope(res[t * COLS:(t + 1) * COLS, n * CH:(n + 1) * CH])
                if row < 0:
                    grad = jnp.where(has_up, grad, 0.0)
                elif row >= ROWS:
                    grad = jnp.where(has_down, grad, 0.0)
                widen(g3, t, row + 1, grad)

    def feat_rows():
        lhs = [
            jnp.concatenate([r3[t, r + 2 + n, :, CH:2 * CH] for n in range(2)], axis=1)
            for r in (0, 2) for t in range(FRAMES)
        ]
        feat[...] = dot(jnp.concatenate(lhs, axis=0), wp[...])

    def back_rows(r):
        return dot(jnp.concatenate([four(g3, t, r) for t in range(FRAMES)], axis=0), wb[...])

    def grad_rows(r, back):
        miss = []
        for t in range(FRAMES):
            at_row = (r + t) * COLS
            goal = jnp.concatenate([tgt[t, r + n].astype(F32) for n in range(2)], axis=1)
            miss.append((feat[at_row:at_row + COLS] - goal).astype(BF16))
        res = back + dot(jnp.concatenate(miss, axis=0), wq[...])
        for n in range(2):
            for t in range(FRAMES):
                grad = res[t * COLS:(t + 1) * COLS, n * CH:(n + 1) * CH] * slp[t, r + n]
                for j, piece in enumerate(shifted(grad)):
                    lane = (t * 3 + 2 - j) * CH
                    p3[(r + n) * COLS:(r + n + 1) * COLS, lane:lane + CH] = piece

    def weight_rows():
        def left(t):
            return jnp.concatenate([xt[t, r:r + 3].reshape(3 * CH, COLS) for r in range(ROWS)], axis=1)

        both = dot(left(0), p3[...])
        late = dot(left(1), p3[:, 3 * CH:])
        for k in range(2):
            for i in range(3):
                for j in range(3):
                    rows, lanes = slice(i * CH, (i + 1) * CH), slice(j * CH, (j + 1) * CH)
                    span = pl.ds(((k * 3 + i) * 3 + j) * CH, CH)
                    if k:
                        buf[span] = both[rows, lanes] + late[rows, lanes]
                    else:
                        buf[span] = both[rows, (3 + j) * CH:(4 + j) * CH]

    def remote(src, dst, send, recv, who):
        cp = pltpu.make_async_remote_copy(
            src_ref=src, dst_ref=dst, send_sem=send, recv_sem=recv,
            device_id=who, device_id_type=MESH,
        )
        cp.start()

    def settle(like, sem):
        pltpu.make_async_copy(like, like, sem).wait()

    ROW, FOUR = xs.at[:, 0], xs.at[:, pl.ds(0, ROWS)]

    @pl.when(home)
    def _():
        for row in range(ROWS):
            pltpu.make_async_copy(lat_hbm.at[:, row], xs.at[:, row + 2], hrecv.at[row]).start()
        pltpu.make_async_copy(tgt_hbm, tgt, tsem).start()

    pl.semaphore_wait(bar, NX * NY - 1 + NZ - 1 + 2 + has_up.astype(jnp.int32) + has_down.astype(jnp.int32))

    def order(c, k):
        return k + c * (ROWS - 1 - 2 * k)

    @pl.when(jnp.logical_not(home))
    def _():
        for k in range(ROWS):
            row = order(1 - core, k)
            remote(lat_hbm.at[:, row], xs.at[:, row + 2], hsend.at[0], hrecv.at[row], partner)
        remote(tgt_hbm, tgt, hsend.at[1], tsem, partner)

    for n in (2, 3, 4):
        loads[n].wait()

    def band(dst, tap):
        dst[...] = jnp.zeros_like(dst)
        for n in range(2):
            for i in range(3):
                for j in range(3):
                    row = ((i + n) * 3 + j) * CH
                    dst[row:row + CH, n * CH:(n + 1) * CH] = tap(i * 3 + j)

    band(wd, lambda k: wdv[k * CH:(k + 1) * CH])
    band(wb, lambda k: wdv[(8 - k) * CH:(9 - k) * CH].T)
    loads[0].wait()
    band(wx, lambda k: wa[k * CH:(k + 1) * CH, :CH])
    loads[1].wait()
    wp[...] = jnp.zeros_like(wp)
    wq[...] = jnp.zeros_like(wq)
    for n in range(2):
        span = slice(n * CH, (n + 1) * CH)
        wp[span, span] = wperc_ref[...]
        wq[span, span] = wperc_ref[...].T

    def pass_on(row):
        settle(ROW, hrecv.at[row])
        if row <= 1:
            @pl.when(has_up)
            def _():
                remote(xs.at[:, row + 2], xs.at[:, row + 6], hsend.at[2], near.at[2 + row], up)
        else:
            @pl.when(has_down)
            def _():
                remote(xs.at[:, row + 2], xs.at[:, row - 2], hsend.at[3], near.at[3 - row], down)
        widen_x(row)

    @pl.when(core == 0)
    def _():
        for row in range(ROWS):
            pass_on(row)

    @pl.when(core == 1)
    def _():
        for row in reversed(range(ROWS)):
            pass_on(row)

    pre_rows(1)

    @pl.when(has_up)
    def _():
        remote(rec.at[1], rhalo.at[1], hsend.at[2], near.at[5], up)

    @pl.when(has_down)
    def _():
        remote(rec.at[0], rhalo.at[0], hsend.at[3], near.at[4], down)

    def arrived(step):
        @pl.when(has_up)
        def _():
            settle(ROW, near.at[(0, 1, 4)[step]])

        @pl.when(has_down)
        def _():
            settle(ROW, near.at[(2, 3, 5)[step]])

    arrived(0)
    widen_x(-1)
    widen_x(ROWS)
    arrived(1)
    widen_x(-2)
    widen_x(ROWS + 1)
    pre_rows(-1)
    pre_rows(ROWS - 1)
    feat_rows()
    disc_rows(1)

    arrived(2)
    for side, row in ((0, -2), (1, ROWS + 1)):
        for t in range(FRAMES):
            widen(r3, t, row + 2, rhalo[side, t].astype(F32))
    disc_rows(-1)
    disc_rows(ROWS - 1)
    back = [back_rows(r) for r in (0, 2)]
    settle(FOUR, tsem)
    for n in range(2):
        grad_rows(2 * n, back[n])
    weight_rows()

    mine, theirs = core * HALF, (1 - core) * HALF
    for g in range(PARTS):
        remote(
            buf.at[pl.ds(pl.multiple_of(theirs + g * PART, 8), PART)],
            cin.at[pl.ds(g * PART, PART)], sent.at[0], crecv.at[g], other,
        )

    def rows_at(base, g, q, size):
        return pl.ds(pl.multiple_of(base + g * PART + q * size, 8), size)

    def in_plane(d):
        return lax.rem(px + d // NY, NX) * NY + lax.rem(py + d % NY, NY)

    def in_line(d):
        return lax.rem(pz + d, NZ)

    class Plane:
        steps, place, who, spot = PLANE, in_plane, plane, px * NY + py

    class Line:
        steps, place, who, spot = LINE, in_line, line, pz

    def route(g):
        if g in LINED:
            return Line, Plane, l1.at[LINED.index(g)], l2.at[LINED.index(g)]
        return Plane, Line, r1.at[g], r2.at[g]

    def add_up(slots):
        total = slots[0]
        for n in range(1, slots.shape[0]):
            total = total + slots[n]
        return total

    for g in range(PARTS):
        first, _, land, _ = route(g)
        size = land.shape[1]
        part = pl.ds(g * PART, PART)
        settle(cin.at[part], crecv.at[g])
        red[part] = buf[pl.ds(pl.multiple_of(mine + g * PART, 8), PART)] + cin[part]
        for d in first.steps:
            remote(
                red.at[rows_at(0, g, first.place(d), size)], land.at[first.spot],
                sent.at[1], v1.at[g], first.who(d),
            )
        land[first.spot] = red[rows_at(0, g, first.spot, size)]
    for g in range(PARTS):
        first, second, land, meet = route(g)
        settle(land.at[pl.ds(0, len(first.steps))], v1.at[g])
        meet[second.spot] = add_up(land)
        for d in second.steps:
            remote(meet.at[second.spot], meet.at[second.spot], sent.at[2], v2.at[g], second.who(d))
    for g in range(PARTS):
        first, second, land, meet = route(g)
        settle(meet.at[pl.ds(0, len(second.steps))], v2.at[g])
        own = rows_at(mine, g, first.spot, land.shape[1])
        out_ref[own] = add_up(meet)
        for d in first.steps:
            remote(out_ref.at[own], out_ref.at[own], sent.at[3], v3.at[g], first.who(d))
    for g in range(PARTS):
        first, _, land, _ = route(g)
        settle(land.at[pl.ds(0, len(first.steps))], v3.at[g])
        rows = pl.ds(pl.multiple_of(mine + g * PART, 8), PART)
        remote(out_ref.at[rows], out_ref.at[rows], sent.at[4], v4, other)
    settle(cin, v4)

    @pl.when(jnp.logical_not(home))
    def _():
        settle(FOUR, hsend.at[0])
        settle(FOUR, hsend.at[1])

    @pl.when(has_up)
    def _():
        settle(xs.at[:, pl.ds(0, 3)], hsend.at[2])

    @pl.when(has_down)
    def _():
        settle(xs.at[:, pl.ds(0, 3)], hsend.at[3])

    settle(cin, sent.at[0])
    outer = (PARTS - len(LINED)) * len(PLANE) * PIECE + len(LINED) * len(LINE) * PART // NZ
    inner = (PARTS - len(LINED)) * len(LINE) * PIECE + len(LINED) * len(PLANE) * PART // NZ
    settle(buf.at[pl.ds(0, outer)], sent.at[1])
    settle(buf.at[pl.ds(0, inner)], sent.at[2])
    settle(buf.at[pl.ds(0, outer)], sent.at[3])
    settle(cin, sent.at[4])


def per_device(latent, target, w_dec, w_disc, w_head, w_perc):
    hbm = pl.BlockSpec(memory_space=pltpu.HBM)
    vmem = pl.BlockSpec(memory_space=pltpu.VMEM)
    dma = pltpu.SemaphoreType.DMA
    plane, line = NX * NY, NZ
    total = pl.pallas_call(
        kernel,
        out_shape=jax.ShapeDtypeStruct((TAPS * CH, CH), F32),
        in_specs=[hbm] * 6,
        out_specs=vmem,
        scratch_shapes=[
            pltpu.VMEM((FRAMES, ROWS + 4, COLS, CH), BF16),
            pltpu.VMEM((FRAMES, ROWS + 4, COLS, 3 * CH), BF16),
            pltpu.VMEM((FRAMES, ROWS + 2, CH, COLS), BF16),
            pltpu.VMEM((FRAMES, ROWS, COLS, CH), BF16),
            pltpu.VMEM((9 * CH, 2 * CH), BF16),
            pltpu.VMEM((12 * CH, 2 * CH), BF16),
            pltpu.VMEM((12 * CH, 2 * CH), BF16),
            pltpu.VMEM((12 * CH, 2 * CH), BF16),
            pltpu.VMEM((2 * CH, 2 * CH), BF16),
            pltpu.VMEM((2 * CH, 2 * CH), BF16),
            pltpu.VMEM((9 * CH, CH), BF16),
            pltpu.VMEM((1, CH), F32),
            pltpu.VMEM((CH, CH), BF16),
            pltpu.VMEM((2, FRAMES, COLS, CH), BF16),
            pltpu.VMEM((2, FRAMES, COLS, CH), BF16),
            pltpu.VMEM((FRAMES, ROWS + 4, COLS, 3 * CH), BF16),
            pltpu.VMEM((FRAMES, ROWS + 2, COLS, 3 * CH), BF16),
            pltpu.VMEM((FRAMES * ROWS * COLS // 2, 2 * CH), F32),
            pltpu.VMEM((FRAMES, ROWS, COLS, CH), F32),
            pltpu.VMEM((ROWS * COLS, FRAMES * 3 * CH), BF16),
            pltpu.VMEM((TAPS * CH, CH), F32),
            pltpu.VMEM((HALF, CH), F32),
            pltpu.VMEM((HALF, CH), F32),
            pltpu.VMEM((PARTS, plane, PIECE, CH), F32),
            pltpu.VMEM((PARTS, line, PIECE, CH), F32),
            pltpu.VMEM((len(LINED), line, PART // NZ, CH), F32),
            pltpu.VMEM((len(LINED), plane, PART // NZ, CH), F32),
            dma((5,)), dma((4,)), dma((ROWS,)), dma((6,)), dma, dma((5,)), dma((PARTS,)),
            dma((PARTS,)), dma((PARTS,)), dma((PARTS,)), dma,
        ],
        compiler_params=pltpu.CompilerParams(
            collective_id=0, has_side_effects=True, vmem_limit_bytes=48 << 20
        ),
        name="tokenizer_step",
    )(
        *(pltpu.with_memory_space_constraint(x, pltpu.HBM) for x in (
            latent[0], target[0], w_dec.reshape(2, 9 * CH, CH), w_disc.reshape(9 * CH, CH),
            w_head.reshape(1, CH), w_perc,
        ))
    )
    pixels = lax.axis_size("dp") * FRAMES * ROWS * lax.axis_size("sect") * COLS
    total = total / jnp.sqrt(jnp.float32(pixels))
    return total.reshape(2, 3, 3, CH, CH)


def solution(mesh):
    in_specs = (
        P("dp", None, "sect", None, None),
        P("dp", None, "sect", None, None),
        P(),
        P(),
        P(),
        P(),
    )
    return jax.shard_map(
        per_device, mesh=mesh, in_specs=in_specs, out_specs=P(), check_vma=False
    )
```

```python
import functools

import jax
import jax.numpy as jnp
from jax import lax
from jax.experimental import pallas as pl
from jax.experimental.pallas import tpu as pltpu
from jax.sharding import PartitionSpec as P

MESH = pl.DeviceIdType.MESH
F32 = jnp.float32
BF16 = jnp.bfloat16
FRAMES, ROWS, COLS, CH = 2, 4, 256, 128
NX, NY, NZ = 4, 4, 8
TAPS = 18
HALF = TAPS * CH // 2
PARTS = 9
LINED = [0, 3, 6]
PART = HALF // PARTS
PIECE = PART // (NX * NY)
PLANE = sorted(range(1, NX * NY), key=lambda d: -min(d // NY, NX - d // NY) - min(d % NY, NY - d % NY))
LINE = sorted(range(1, NZ), key=lambda d: -min(d, NZ - d))


def slope(value):
    sig = jax.nn.sigmoid(value)
    return sig * (1.0 + value * (1.0 - sig))


def shifted(tile):
    at = lax.broadcasted_iota(jnp.int32, tile.shape, 0)
    before = jnp.where(at == 0, 0.0, pltpu.roll(tile, 1, 0))
    after = jnp.where(at == COLS - 1, 0.0, pltpu.roll(tile, COLS - 1, 0))
    return before.astype(BF16), tile.astype(BF16), after.astype(BF16)


def dot(a, b):
    return jnp.dot(a, b, preferred_element_type=F32)


def kernel(
    lat_hbm, tgt_hbm, wdec_hbm, wdisc_hbm, whead_hbm, wperc_hbm,
    out_ref,
    xs, x3, xt, tgt, wa, wx, wd, wb, wp, wq, wdv, whead_ref, wperc_ref, rec, rhalo, r3, g3, feat, slp, p3,
    buf, cin, red, r1, r2, l1, l2,
    lsem, hsend, hrecv, near, tsem, sent, crecv, v1, v2, v3, v4,
):
    dp, sect = lax.axis_index("dp"), lax.axis_index("sect")
    core, px = lax.rem(dp, 2), lax.rem(dp // 2, NX)
    py, pz = sect // 2, (dp // 8) * 2 + lax.rem(sect, 2)

    def at(x, y, z, c):
        return ((z // 2) * 8 + x * 2 + c, y * 2 + lax.rem(z, 2))

    other = at(px, py, pz, 1 - core)

    def plane(d):
        return at(lax.rem(px + d // NY, NX), lax.rem(py + d % NY, NY), pz, core)

    def line(d):
        return at(px, py, lax.rem(pz + d, NZ), core)

    low = lax.rem(pz, 2)
    home = low == core
    block = 2 * py + core
    has_up, has_down = block > 0, block < 2 * NY - 1
    partner = at(px, py, pz + 1 - 2 * low, 1 - core)
    up = at(px, py - (1 - core), pz, 1 - core)
    down = at(px, py + core, pz, 1 - core)

    bar = pltpu.get_barrier_semaphore()

    def greet(who):
        pl.semaphore_signal(bar, inc=1, device_id=who, device_id_type=MESH)

    greet(partner)

    @pl.when(has_up)
    def _():
        greet(up)

    @pl.when(has_down)
    def _():
        greet(down)

    greet(other)
    for d in range(1, NX * NY):
        greet(plane(d))
    for d in range(1, NZ):
        greet(line(d))

    loads = [
        pltpu.make_async_copy(wdec_hbm.at[1], wa.at[:, pl.ds(0, CH)], lsem.at[0]),
        pltpu.make_async_copy(wdec_hbm.at[0], wa.at[:, pl.ds(CH, CH)], lsem.at[1]),
        pltpu.make_async_copy(wdisc_hbm, wdv, lsem.at[2]),
        pltpu.make_async_copy(wperc_hbm, wperc_ref, lsem.at[3]),
        pltpu.make_async_copy(whead_hbm, whead_ref, lsem.at[4]),
    ]
    for cp in loads:
        cp.start()

    zrow = jnp.zeros((FRAMES, COLS, CH), BF16)

    @pl.when(jnp.logical_not(has_up))
    def _():
        xs[:, 0] = zrow
        xs[:, 1] = zrow
        rhalo[0] = zrow

    @pl.when(jnp.logical_not(has_down))
    def _():
        xs[:, 6] = zrow
        xs[:, 7] = zrow
        rhalo[1] = zrow

    def widen(dst, t, idx, tile):
        for j, piece in enumerate(shifted(tile)):
            dst[t, idx, :, j * CH:(j + 1) * CH] = piece

    def widen_x(row):
        for t in range(FRAMES):
            tile = xs[t, row + 2]
            widen(x3, t, row + 2, tile.astype(F32))
            if -1 <= row <= ROWS:
                xt[t, row + 1] = tile.T

    def around(src, t, idx):
        return jnp.concatenate([src[t, idx - 1], src[t, idx], src[t, idx + 1]], axis=1)

    def four(src, t, idx):
        return jnp.concatenate([src[t, idx + q] for q in range(4)], axis=1)

    def pre_rows(r):
        first = dot(jnp.concatenate([around(x3, 0, r + 2 + n) for n in range(2)], axis=0), wa[...])
        second = dot(four(x3, 1, r + 1), wx[...])
        for n in range(2):
            row, span = r + n, slice(n * COLS, (n + 1) * COLS)
            for t in range(FRAMES):
                pre = first[span, :CH] if t == 0 else first[span, CH:] + second[:, n * CH:(n + 1) * CH]
                sig = jax.nn.sigmoid(pre)
                value = pre * sig
                if row < 0:
                    value = jnp.where(has_up, value, 0.0)
                elif row >= ROWS:
                    value = jnp.where(has_down, value, 0.0)
                else:
                    slp[t, row] = sig * (1.0 + pre * (1.0 - sig))
                widen(r3, t, row + 2, value)
                if row in (1, 2):
                    rec[2 - row, t] = value.astype(BF16)

    def disc_rows(r):
        res = dot(jnp.concatenate([four(r3, t, r + 1) for t in range(FRAMES)], axis=0), wd[...])
        for n in range(2):
            row = r + n
            for t in range(FRAMES):
                grad = -whead_ref[...] * slope(res[t * COLS:(t + 1) * COLS, n * CH:(n + 1) * CH])
                if row < 0:
                    grad = jnp.where(has_up, grad, 0.0)
                elif row >= ROWS:
                    grad = jnp.where(has_down, grad, 0.0)
                widen(g3, t, row + 1, grad)

    def feat_rows():
        lhs = [
            jnp.concatenate([r3[t, r + 2 + n, :, CH:2 * CH] for n in range(2)], axis=1)
            for r in (0, 2) for t in range(FRAMES)
        ]
        feat[...] = dot(jnp.concatenate(lhs, axis=0), wp[...])

    def back_rows(r):
        return dot(jnp.concatenate([four(g3, t, r) for t in range(FRAMES)], axis=0), wb[...])

    def grad_rows(r, back):
        miss = []
        for t in range(FRAMES):
            at_row = (r + t) * COLS
            goal = jnp.concatenate([tgt[t, r + n].astype(F32) for n in range(2)], axis=1)
            miss.append((feat[at_row:at_row + COLS] - goal).astype(BF16))
        res = back + dot(jnp.concatenate(miss, axis=0), wq[...])
        for n in range(2):
            for t in range(FRAMES):
                grad = res[t * COLS:(t + 1) * COLS, n * CH:(n + 1) * CH] * slp[t, r + n]
                for j, piece in enumerate(shifted(grad)):
                    lane = (t * 3 + 2 - j) * CH
                    p3[(r + n) * COLS:(r + n + 1) * COLS, lane:lane + CH] = piece

    def weight_rows():
        def left(t):
            return jnp.concatenate([xt[t, r:r + 3].reshape(3 * CH, COLS) for r in range(ROWS)], axis=1)

        both = dot(left(0), p3[...])
        late = dot(left(1), p3[:, 3 * CH:])
        for k in range(2):
            for i in range(3):
                for j in range(3):
                    rows, lanes = slice(i * CH, (i + 1) * CH), slice(j * CH, (j + 1) * CH)
                    span = pl.ds(((k * 3 + i) * 3 + j) * CH, CH)
                    if k:
                        buf[span] = both[rows, lanes] + late[rows, lanes]
                    else:
                        buf[span] = both[rows, (3 + j) * CH:(4 + j) * CH]

    def remote(src, dst, send, recv, who):
        cp = pltpu.make_async_remote_copy(
            src_ref=src, dst_ref=dst, send_sem=send, recv_sem=recv,
            device_id=who, device_id_type=MESH,
        )
        cp.start()

    def settle(like, sem):
        pltpu.make_async_copy(like, like, sem).wait()

    ROW, FOUR = xs.at[:, 0], xs.at[:, pl.ds(0, ROWS)]

    @pl.when(home)
    def _():
        for row in range(ROWS):
            pltpu.make_async_copy(lat_hbm.at[:, row], xs.at[:, row + 2], hrecv.at[row]).start()
        pltpu.make_async_copy(tgt_hbm, tgt, tsem).start()

    for n in (2, 3, 4):
        loads[n].wait()

    def band(dst, tap):
        dst[...] = jnp.zeros_like(dst)
        for n in range(2):
            for i in range(3):
                for j in range(3):
                    row = ((i + n) * 3 + j) * CH
                    dst[row:row + CH, n * CH:(n + 1) * CH] = tap(i * 3 + j)

    band(wd, lambda k: wdv[k * CH:(k + 1) * CH])
    band(wb, lambda k: wdv[(8 - k) * CH:(9 - k) * CH].T)
    loads[0].wait()
    band(wx, lambda k: wa[k * CH:(k + 1) * CH, :CH])
    loads[1].wait()
    wp[...] = jnp.zeros_like(wp)
    wq[...] = jnp.zeros_like(wq)
    for n in range(2):
        span = slice(n * CH, (n + 1) * CH)
        wp[span, span] = wperc_ref[...]
        wq[span, span] = wperc_ref[...].T

    pl.semaphore_wait(bar, NX * NY - 1 + NZ - 1 + 2 + has_up.astype(jnp.int32) + has_down.astype(jnp.int32))

    def order(c, k):
        return k + c * (ROWS - 1 - 2 * k)

    @pl.when(jnp.logical_not(home))
    def _():
        for k in range(ROWS):
            row = order(1 - core, k)
            remote(lat_hbm.at[:, row], xs.at[:, row + 2], hsend.at[0], hrecv.at[row], partner)
        remote(tgt_hbm, tgt, hsend.at[1], tsem, partner)

    def pass_on(row):
        settle(ROW, hrecv.at[row])
        if row <= 1:
            @pl.when(has_up)
            def _():
                remote(xs.at[:, row + 2], xs.at[:, row + 6], hsend.at[2], near.at[2 + row], up)
        else:
            @pl.when(has_down)
            def _():
                remote(xs.at[:, row + 2], xs.at[:, row - 2], hsend.at[3], near.at[3 - row], down)
        widen_x(row)

    @pl.when(core == 0)
    def _():
        for row in range(ROWS):
            pass_on(row)

    @pl.when(core == 1)
    def _():
        for row in reversed(range(ROWS)):
            pass_on(row)

    pre_rows(1)

    @pl.when(has_up)
    def _():
        remote(rec.at[1], rhalo.at[1], hsend.at[2], near.at[5], up)

    @pl.when(has_down)
    def _():
        remote(rec.at[0], rhalo.at[0], hsend.at[3], near.at[4], down)

    def arrived(step):
        @pl.when(has_up)
        def _():
            settle(ROW, near.at[(0, 1, 4)[step]])

        @pl.when(has_down)
        def _():
            settle(ROW, near.at[(2, 3, 5)[step]])

    arrived(0)
    widen_x(-1)
    widen_x(ROWS)
    arrived(1)
    widen_x(-2)
    widen_x(ROWS + 1)
    pre_rows(-1)
    pre_rows(ROWS - 1)
    feat_rows()
    disc_rows(1)

    arrived(2)
    for side, row in ((0, -2), (1, ROWS + 1)):
        for t in range(FRAMES):
            widen(r3, t, row + 2, rhalo[side, t].astype(F32))
    disc_rows(-1)
    disc_rows(ROWS - 1)
    back = [back_rows(r) for r in (0, 2)]
    settle(FOUR, tsem)
    for n in range(2):
        grad_rows(2 * n, back[n])
    weight_rows()

    mine, theirs = core * HALF, (1 - core) * HALF
    for g in range(PARTS):
        remote(
            buf.at[pl.ds(pl.multiple_of(theirs + g * PART, 8), PART)],
            cin.at[pl.ds(g * PART, PART)], sent.at[0], crecv.at[g], other,
        )

    def rows_at(base, g, q, size):
        return pl.ds(pl.multiple_of(base + g * PART + q * size, 8), size)

    def in_plane(d):
        return lax.rem(px + d // NY, NX) * NY + lax.rem(py + d % NY, NY)

    def in_line(d):
        return lax.rem(pz + d, NZ)

    class Plane:
        steps, place, who, spot = PLANE, in_plane, plane, px * NY + py

    class Line:
        steps, place, who, spot = LINE, in_line, line, pz

    def route(g):
        if g in LINED:
            return Line, Plane, l1.at[LINED.index(g)], l2.at[LINED.index(g)]
        return Plane, Line, r1.at[g], r2.at[g]

    def turned(group, g):
        if g % 2 == 0:
            return group.steps
        if group is Line:
            return [NZ - d for d in group.steps]
        return [(NX - d // NY) % NX * NY + (NY - d % NY) % NY for d in group.steps]

    def add_up(slots):
        total = slots[0]
        for n in range(1, slots.shape[0]):
            total = total + slots[n]
        return total

    for g in range(PARTS):
        first, _, land, _ = route(g)
        size = land.shape[1]
        part = pl.ds(g * PART, PART)
        settle(cin.at[part], crecv.at[g])
        red[part] = buf[pl.ds(pl.multiple_of(mine + g * PART, 8), PART)] + cin[part]
        for d in turned(first, g):
            remote(
                red.at[rows_at(0, g, first.place(d), size)], land.at[first.spot],
                sent.at[1], v1.at[g], first.who(d),
            )
        land[first.spot] = red[rows_at(0, g, first.spot, size)]
    for g in range(PARTS):
        first, second, land, meet = route(g)
        settle(land.at[pl.ds(0, len(first.steps))], v1.at[g])
        meet[second.spot] = add_up(land)
        for d in turned(second, g):
            remote(meet.at[second.spot], meet.at[second.spot], sent.at[2], v2.at[g], second.who(d))
    for g in range(PARTS):
        first, second, land, meet = route(g)
        settle(meet.at[pl.ds(0, len(second.steps))], v2.at[g])
        own = rows_at(mine, g, first.spot, land.shape[1])
        out_ref[own] = add_up(meet)
        for d in turned(first, g):
            remote(out_ref.at[own], out_ref.at[own], sent.at[3], v3.at[g], first.who(d))
    for g in range(PARTS):
        first, _, land, _ = route(g)
        settle(land.at[pl.ds(0, len(first.steps))], v3.at[g])
        rows = pl.ds(pl.multiple_of(mine + g * PART, 8), PART)
        remote(out_ref.at[rows], out_ref.at[rows], sent.at[4], v4, other)
    settle(cin, v4)

    @pl.when(jnp.logical_not(home))
    def _():
        settle(FOUR, hsend.at[0])
        settle(FOUR, hsend.at[1])

    @pl.when(has_up)
    def _():
        settle(xs.at[:, pl.ds(0, 3)], hsend.at[2])

    @pl.when(has_down)
    def _():
        settle(xs.at[:, pl.ds(0, 3)], hsend.at[3])

    settle(cin, sent.at[0])
    outer = (PARTS - len(LINED)) * len(PLANE) * PIECE + len(LINED) * len(LINE) * PART // NZ
    inner = (PARTS - len(LINED)) * len(LINE) * PIECE + len(LINED) * len(PLANE) * PART // NZ
    settle(buf.at[pl.ds(0, outer)], sent.at[1])
    settle(buf.at[pl.ds(0, inner)], sent.at[2])
    settle(buf.at[pl.ds(0, outer)], sent.at[3])
    settle(cin, sent.at[4])


def per_device(latent, target, w_dec, w_disc, w_head, w_perc):
    hbm = pl.BlockSpec(memory_space=pltpu.HBM)
    vmem = pl.BlockSpec(memory_space=pltpu.VMEM)
    dma = pltpu.SemaphoreType.DMA
    plane, line = NX * NY, NZ
    total = pl.pallas_call(
        kernel,
        out_shape=jax.ShapeDtypeStruct((TAPS * CH, CH), F32),
        in_specs=[hbm] * 6,
        out_specs=vmem,
        scratch_shapes=[
            pltpu.VMEM((FRAMES, ROWS + 4, COLS, CH), BF16),
            pltpu.VMEM((FRAMES, ROWS + 4, COLS, 3 * CH), BF16),
            pltpu.VMEM((FRAMES, ROWS + 2, CH, COLS), BF16),
            pltpu.VMEM((FRAMES, ROWS, COLS, CH), BF16),
            pltpu.VMEM((9 * CH, 2 * CH), BF16),
            pltpu.VMEM((12 * CH, 2 * CH), BF16),
            pltpu.VMEM((12 * CH, 2 * CH), BF16),
            pltpu.VMEM((12 * CH, 2 * CH), BF16),
            pltpu.VMEM((2 * CH, 2 * CH), BF16),
            pltpu.VMEM((2 * CH, 2 * CH), BF16),
            pltpu.VMEM((9 * CH, CH), BF16),
            pltpu.VMEM((1, CH), F32),
            pltpu.VMEM((CH, CH), BF16),
            pltpu.VMEM((2, FRAMES, COLS, CH), BF16),
            pltpu.VMEM((2, FRAMES, COLS, CH), BF16),
            pltpu.VMEM((FRAMES, ROWS + 4, COLS, 3 * CH), BF16),
            pltpu.VMEM((FRAMES, ROWS + 2, COLS, 3 * CH), BF16),
            pltpu.VMEM((FRAMES * ROWS * COLS // 2, 2 * CH), F32),
            pltpu.VMEM((FRAMES, ROWS, COLS, CH), F32),
            pltpu.VMEM((ROWS * COLS, FRAMES * 3 * CH), BF16),
            pltpu.VMEM((TAPS * CH, CH), F32),
            pltpu.VMEM((HALF, CH), F32),
            pltpu.VMEM((HALF, CH), F32),
            pltpu.VMEM((PARTS, plane, PIECE, CH), F32),
            pltpu.VMEM((PARTS, line, PIECE, CH), F32),
            pltpu.VMEM((len(LINED), line, PART // NZ, CH), F32),
            pltpu.VMEM((len(LINED), plane, PART // NZ, CH), F32),
            dma((5,)), dma((4,)), dma((ROWS,)), dma((6,)), dma, dma((5,)), dma((PARTS,)),
            dma((PARTS,)), dma((PARTS,)), dma((PARTS,)), dma,
        ],
        compiler_params=pltpu.CompilerParams(
            collective_id=0, has_side_effects=True, vmem_limit_bytes=48 << 20
        ),
        name="tokenizer_step",
    )(
        *(pltpu.with_memory_space_constraint(x, pltpu.HBM) for x in (
            latent[0], target[0], w_dec.reshape(2, 9 * CH, CH), w_disc.reshape(9 * CH, CH),
            w_head.reshape(1, CH), w_perc,
        ))
    )
    pixels = lax.axis_size("dp") * FRAMES * ROWS * lax.axis_size("sect") * COLS
    total = total / jnp.sqrt(jnp.float32(pixels))
    return total.reshape(2, 3, 3, CH, CH)


def solution(mesh):
    in_specs = (
        P("dp", None, "sect", None, None),
        P("dp", None, "sect", None, None),
        P(),
        P(),
        P(),
        P(),
    )
    return jax.shard_map(
        per_device, mesh=mesh, in_specs=in_specs, out_specs=P(), check_vma=False
    )
```

```python
import functools

import jax
import jax.numpy as jnp
from jax import lax
from jax.experimental import pallas as pl
from jax.experimental.pallas import tpu as pltpu
from jax.sharding import PartitionSpec as P

MESH = pl.DeviceIdType.MESH
F32 = jnp.float32
BF16 = jnp.bfloat16
FRAMES, ROWS, COLS, CH = 2, 4, 256, 128
NX, NY, NZ = 4, 4, 8
TAPS = 18
HALF = TAPS * CH // 2
LINED = [0, 2, 4]
PLANED = [1, 3, 5]
SIZES = [128, 256, 128, 256, 128, 256]
PARTS = len(SIZES)
STARTS = [sum(SIZES[:g]) for g in range(PARTS)]
PIECE = SIZES[PLANED[0]] // (NX * NY)
STRIP = SIZES[LINED[0]] // NZ
PLANE = sorted(range(1, NX * NY), key=lambda d: -min(d // NY, NX - d // NY) - min(d % NY, NY - d % NY))
LINE = sorted(range(1, NZ), key=lambda d: -min(d, NZ - d))


def slope(value):
    sig = jax.nn.sigmoid(value)
    return sig * (1.0 + value * (1.0 - sig))


def shifted(tile):
    at = lax.broadcasted_iota(jnp.int32, tile.shape, 0)
    before = jnp.where(at == 0, 0.0, pltpu.roll(tile, 1, 0))
    after = jnp.where(at == COLS - 1, 0.0, pltpu.roll(tile, COLS - 1, 0))
    return before.astype(BF16), tile.astype(BF16), after.astype(BF16)


def dot(a, b):
    return jnp.dot(a, b, preferred_element_type=F32)


def kernel(
    lat_hbm, tgt_hbm, wdec_hbm, wdisc_hbm, whead_hbm, wperc_hbm,
    out_ref,
    xs, x3, xt, tgt, wa, wx, wd, wb, wp, wq, wdv, whead_ref, wperc_ref, rec, rhalo, r3, g3, feat, slp, p3,
    buf, cin, red, r1, r2, l1, l2,
    lsem, hsend, hrecv, near, tsem, sent, crecv, v1, v2, v3, v4,
):
    dp, sect = lax.axis_index("dp"), lax.axis_index("sect")
    core, px = lax.rem(dp, 2), lax.rem(dp // 2, NX)
    py, pz = sect // 2, (dp // 8) * 2 + lax.rem(sect, 2)

    def at(x, y, z, c):
        return ((z // 2) * 8 + x * 2 + c, y * 2 + lax.rem(z, 2))

    other = at(px, py, pz, 1 - core)

    def plane(d):
        return at(lax.rem(px + d // NY, NX), lax.rem(py + d % NY, NY), pz, core)

    def line(d):
        return at(px, py, lax.rem(pz + d, NZ), core)

    low = lax.rem(pz, 2)
    home = low == core
    block = 2 * py + core
    has_up, has_down = block > 0, block < 2 * NY - 1
    partner = at(px, py, pz + 1 - 2 * low, 1 - core)
    up = at(px, py - (1 - core), pz, 1 - core)
    down = at(px, py + core, pz, 1 - core)

    bar = pltpu.get_barrier_semaphore()

    def greet(who):
        pl.semaphore_signal(bar, inc=1, device_id=who, device_id_type=MESH)

    @pl.when(has_up)
    def _():
        greet(up)

    @pl.when(has_down)
    def _():
        greet(down)

    greet(partner)
    greet(other)
    for d in range(1, NX * NY):
        greet(plane(d))
    for d in range(1, NZ):
        greet(line(d))

    loads = [
        pltpu.make_async_copy(wdec_hbm.at[1], wa.at[:, pl.ds(0, CH)], lsem.at[0]),
        pltpu.make_async_copy(wdec_hbm.at[0], wa.at[:, pl.ds(CH, CH)], lsem.at[1]),
        pltpu.make_async_copy(wdisc_hbm, wdv, lsem.at[2]),
        pltpu.make_async_copy(wperc_hbm, wperc_ref, lsem.at[3]),
        pltpu.make_async_copy(whead_hbm, whead_ref, lsem.at[4]),
    ]
    for cp in loads:
        cp.start()

    zrow = jnp.zeros((FRAMES, COLS, CH), BF16)

    @pl.when(jnp.logical_not(has_up))
    def _():
        xs[:, 0] = zrow
        xs[:, 1] = zrow
        rhalo[0] = zrow

    @pl.when(jnp.logical_not(has_down))
    def _():
        xs[:, 6] = zrow
        xs[:, 7] = zrow
        rhalo[1] = zrow

    def widen(dst, t, idx, tile):
        for j, piece in enumerate(shifted(tile)):
            dst[t, idx, :, j * CH:(j + 1) * CH] = piece

    def widen_x(row):
        for t in range(FRAMES):
            tile = xs[t, row + 2]
            widen(x3, t, row + 2, tile.astype(F32))
            if -1 <= row <= ROWS:
                xt[t, row + 1] = tile.T

    def around(src, t, idx):
        return jnp.concatenate([src[t, idx - 1], src[t, idx], src[t, idx + 1]], axis=1)

    def four(src, t, idx):
        return jnp.concatenate([src[t, idx + q] for q in range(4)], axis=1)

    def pre_rows(r):
        first = dot(jnp.concatenate([around(x3, 0, r + 2 + n) for n in range(2)], axis=0), wa[...])
        second = dot(four(x3, 1, r + 1), wx[...])
        for n in range(2):
            row, span = r + n, slice(n * COLS, (n + 1) * COLS)
            for t in range(FRAMES):
                pre = first[span, :CH] if t == 0 else first[span, CH:] + second[:, n * CH:(n + 1) * CH]
                sig = jax.nn.sigmoid(pre)
                value = pre * sig
                if row < 0:
                    value = jnp.where(has_up, value, 0.0)
                elif row >= ROWS:
                    value = jnp.where(has_down, value, 0.0)
                else:
                    slp[t, row] = sig * (1.0 + pre * (1.0 - sig))
                widen(r3, t, row + 2, value)
                if row in (1, 2):
                    rec[2 - row, t] = value.astype(BF16)

    def disc_rows(r):
        res = dot(jnp.concatenate([four(r3, t, r + 1) for t in range(FRAMES)], axis=0), wd[...])
        for n in range(2):
            row = r + n
            for t in range(FRAMES):
                grad = -whead_ref[...] * slope(res[t * COLS:(t + 1) * COLS, n * CH:(n + 1) * CH])
                if row < 0:
                    grad = jnp.where(has_up, grad, 0.0)
                elif row >= ROWS:
                    grad = jnp.where(has_down, grad, 0.0)
                widen(g3, t, row + 1, grad)

    def feat_rows():
        lhs = [
            jnp.concatenate([r3[t, r + 2 + n, :, CH:2 * CH] for n in range(2)], axis=1)
            for r in (0, 2) for t in range(FRAMES)
        ]
        feat[...] = dot(jnp.concatenate(lhs, axis=0), wp[...])

    def back_rows(r):
        return dot(jnp.concatenate([four(g3, t, r) for t in range(FRAMES)], axis=0), wb[...])

    def grad_rows(r, back):
        miss = []
        for t in range(FRAMES):
            at_row = (r + t) * COLS
            goal = jnp.concatenate([tgt[t, r + n].astype(F32) for n in range(2)], axis=1)
            miss.append((feat[at_row:at_row + COLS] - goal).astype(BF16))
        res = back + dot(jnp.concatenate(miss, axis=0), wq[...])
        for n in range(2):
            for t in range(FRAMES):
                grad = res[t * COLS:(t + 1) * COLS, n * CH:(n + 1) * CH] * slp[t, r + n]
                for j, piece in enumerate(shifted(grad)):
                    lane = (t * 3 + 2 - j) * CH
                    p3[(r + n) * COLS:(r + n + 1) * COLS, lane:lane + CH] = piece

    def weight_rows():
        def left(t):
            return jnp.concatenate([xt[t, r:r + 3].reshape(3 * CH, COLS) for r in range(ROWS)], axis=1)

        both = dot(left(0), p3[...])
        late = dot(left(1), p3[:, 3 * CH:])
        for k in range(2):
            for i in range(3):
                for j in range(3):
                    rows, lanes = slice(i * CH, (i + 1) * CH), slice(j * CH, (j + 1) * CH)
                    span = pl.ds(((k * 3 + i) * 3 + j) * CH, CH)
                    if k:
                        buf[span] = both[rows, lanes] + late[rows, lanes]
                    else:
                        buf[span] = both[rows, (3 + j) * CH:(4 + j) * CH]

    def remote(src, dst, send, recv, who):
        cp = pltpu.make_async_remote_copy(
            src_ref=src, dst_ref=dst, send_sem=send, recv_sem=recv,
            device_id=who, device_id_type=MESH,
        )
        cp.start()

    def settle(like, sem):
        pltpu.make_async_copy(like, like, sem).wait()

    ROW, FOUR = xs.at[:, 0], xs.at[:, pl.ds(0, ROWS)]

    @pl.when(home)
    def _():
        for row in range(ROWS):
            pltpu.make_async_copy(lat_hbm.at[:, row], xs.at[:, row + 2], hrecv.at[row]).start()
        pltpu.make_async_copy(tgt_hbm, tgt, tsem).start()

    pl.semaphore_wait(bar, NX * NY - 1 + NZ - 1 + 2 + has_up.astype(jnp.int32) + has_down.astype(jnp.int32))

    def order(c, k):
        return k + c * (ROWS - 1 - 2 * k)

    @pl.when(jnp.logical_not(home))
    def _():
        for k in range(ROWS):
            row = order(1 - core, k)
            remote(lat_hbm.at[:, row], xs.at[:, row + 2], hsend.at[0], hrecv.at[row], partner)
        remote(tgt_hbm, tgt, hsend.at[1], tsem, partner)

    for n in (2, 3, 4):
        loads[n].wait()

    def band(dst, tap):
        dst[...] = jnp.zeros_like(dst)
        for n in range(2):
            for i in range(3):
                for j in range(3):
                    row = ((i + n) * 3 + j) * CH
                    dst[row:row + CH, n * CH:(n + 1) * CH] = tap(i * 3 + j)

    band(wd, lambda k: wdv[k * CH:(k + 1) * CH])
    band(wb, lambda k: wdv[(8 - k) * CH:(9 - k) * CH].T)
    loads[0].wait()
    band(wx, lambda k: wa[k * CH:(k + 1) * CH, :CH])
    loads[1].wait()
    wp[...] = jnp.zeros_like(wp)
    wq[...] = jnp.zeros_like(wq)
    for n in range(2):
        span = slice(n * CH, (n + 1) * CH)
        wp[span, span] = wperc_ref[...]
        wq[span, span] = wperc_ref[...].T

    def pass_on(row):
        settle(ROW, hrecv.at[row])
        if row <= 1:
            @pl.when(has_up)
            def _():
                remote(xs.at[:, row + 2], xs.at[:, row + 6], hsend.at[2], near.at[2 + row], up)
        else:
            @pl.when(has_down)
            def _():
                remote(xs.at[:, row + 2], xs.at[:, row - 2], hsend.at[3], near.at[3 - row], down)
        widen_x(row)

    @pl.when(core == 0)
    def _():
        for row in range(ROWS):
            pass_on(row)

    @pl.when(core == 1)
    def _():
        for row in reversed(range(ROWS)):
            pass_on(row)

    pre_rows(1)

    @pl.when(has_up)
    def _():
        remote(rec.at[1], rhalo.at[1], hsend.at[2], near.at[5], up)

    @pl.when(has_down)
    def _():
        remote(rec.at[0], rhalo.at[0], hsend.at[3], near.at[4], down)

    def arrived(step):
        @pl.when(has_up)
        def _():
            settle(ROW, near.at[(0, 1, 4)[step]])

        @pl.when(has_down)
        def _():
            settle(ROW, near.at[(2, 3, 5)[step]])

    arrived(0)
    widen_x(-1)
    widen_x(ROWS)
    arrived(1)
    widen_x(-2)
    widen_x(ROWS + 1)
    pre_rows(-1)
    pre_rows(ROWS - 1)
    feat_rows()
    disc_rows(1)

    arrived(2)
    for side, row in ((0, -2), (1, ROWS + 1)):
        for t in range(FRAMES):
            widen(r3, t, row + 2, rhalo[side, t].astype(F32))
    disc_rows(-1)
    disc_rows(ROWS - 1)
    back = [back_rows(r) for r in (0, 2)]
    settle(FOUR, tsem)
    for n in range(2):
        grad_rows(2 * n, back[n])
    weight_rows()

    mine, theirs = core * HALF, (1 - core) * HALF
    for g in range(PARTS):
        remote(
            buf.at[pl.ds(pl.multiple_of(theirs + STARTS[g], 8), SIZES[g])],
            cin.at[pl.ds(STARTS[g], SIZES[g])], sent.at[0], crecv.at[g], other,
        )

    def rows_at(base, g, q, size):
        return pl.ds(pl.multiple_of(base + STARTS[g] + q * size, 8), size)

    def in_plane(d):
        return lax.rem(px + d // NY, NX) * NY + lax.rem(py + d % NY, NY)

    def in_line(d):
        return lax.rem(pz + d, NZ)

    class Plane:
        steps, place, who, spot = PLANE, in_plane, plane, px * NY + py

    class Line:
        steps, place, who, spot = LINE, in_line, line, pz

    def route(g):
        if g in LINED:
            return Line, Plane, l1.at[LINED.index(g)], l2.at[LINED.index(g)]
        return Plane, Line, r1.at[PLANED.index(g)], r2.at[PLANED.index(g)]

    def turned(group, g):
        if g % 2 == 0:
            return group.steps
        if group is Line:
            return [NZ - d for d in group.steps]
        return [(NX - d // NY) % NX * NY + (NY - d % NY) % NY for d in group.steps]

    def add_up(slots):
        total = slots[0]
        for n in range(1, slots.shape[0]):
            total = total + slots[n]
        return total

    for g in range(PARTS):
        first, _, land, _ = route(g)
        size = land.shape[1]
        part = pl.ds(STARTS[g], SIZES[g])
        settle(cin.at[part], crecv.at[g])
        red[part] = buf[pl.ds(pl.multiple_of(mine + STARTS[g], 8), SIZES[g])] + cin[part]
        for d in turned(first, g):
            remote(
                red.at[rows_at(0, g, first.place(d), size)], land.at[first.spot],
                sent.at[1], v1.at[g], first.who(d),
            )
        land[first.spot] = red[rows_at(0, g, first.spot, size)]
    for g in range(PARTS):
        first, second, land, meet = route(g)
        settle(land.at[pl.ds(0, len(first.steps))], v1.at[g])
        meet[second.spot] = add_up(land)
        for d in turned(second, g):
            remote(meet.at[second.spot], meet.at[second.spot], sent.at[2], v2.at[g], second.who(d))
    for g in range(PARTS):
        first, second, land, meet = route(g)
        settle(meet.at[pl.ds(0, len(second.steps))], v2.at[g])
        own = rows_at(mine, g, first.spot, land.shape[1])
        out_ref[own] = add_up(meet)
        for d in turned(first, g):
            remote(out_ref.at[own], out_ref.at[own], sent.at[3], v3.at[g], first.who(d))
    for g in range(PARTS):
        first, _, land, _ = route(g)
        settle(land.at[pl.ds(0, len(first.steps))], v3.at[g])
        rows = pl.ds(pl.multiple_of(mine + STARTS[g], 8), SIZES[g])
        remote(out_ref.at[rows], out_ref.at[rows], sent.at[4], v4, other)
    settle(cin, v4)

    @pl.when(jnp.logical_not(home))
    def _():
        settle(FOUR, hsend.at[0])
        settle(FOUR, hsend.at[1])

    @pl.when(has_up)
    def _():
        settle(xs.at[:, pl.ds(0, 3)], hsend.at[2])

    @pl.when(has_down)
    def _():
        settle(xs.at[:, pl.ds(0, 3)], hsend.at[3])

    settle(cin, sent.at[0])
    outer = (PARTS - len(LINED)) * len(PLANE) * PIECE + len(LINED) * len(LINE) * STRIP
    inner = (PARTS - len(LINED)) * len(LINE) * PIECE + len(LINED) * len(PLANE) * STRIP
    settle(buf.at[pl.ds(0, outer)], sent.at[1])
    settle(buf.at[pl.ds(0, inner)], sent.at[2])
    settle(buf.at[pl.ds(0, outer)], sent.at[3])
    settle(cin, sent.at[4])


def per_device(latent, target, w_dec, w_disc, w_head, w_perc):
    hbm = pl.BlockSpec(memory_space=pltpu.HBM)
    vmem = pl.BlockSpec(memory_space=pltpu.VMEM)
    dma = pltpu.SemaphoreType.DMA
    plane, line = NX * NY, NZ
    total = pl.pallas_call(
        kernel,
        out_shape=jax.ShapeDtypeStruct((TAPS * CH, CH), F32),
        in_specs=[hbm] * 6,
        out_specs=vmem,
        scratch_shapes=[
            pltpu.VMEM((FRAMES, ROWS + 4, COLS, CH), BF16),
            pltpu.VMEM((FRAMES, ROWS + 4, COLS, 3 * CH), BF16),
            pltpu.VMEM((FRAMES, ROWS + 2, CH, COLS), BF16),
            pltpu.VMEM((FRAMES, ROWS, COLS, CH), BF16),
            pltpu.VMEM((9 * CH, 2 * CH), BF16),
            pltpu.VMEM((12 * CH, 2 * CH), BF16),
            pltpu.VMEM((12 * CH, 2 * CH), BF16),
            pltpu.VMEM((12 * CH, 2 * CH), BF16),
            pltpu.VMEM((2 * CH, 2 * CH), BF16),
            pltpu.VMEM((2 * CH, 2 * CH), BF16),
            pltpu.VMEM((9 * CH, CH), BF16),
            pltpu.VMEM((1, CH), F32),
            pltpu.VMEM((CH, CH), BF16),
            pltpu.VMEM((2, FRAMES, COLS, CH), BF16),
            pltpu.VMEM((2, FRAMES, COLS, CH), BF16),
            pltpu.VMEM((FRAMES, ROWS + 4, COLS, 3 * CH), BF16),
            pltpu.VMEM((FRAMES, ROWS + 2, COLS, 3 * CH), BF16),
            pltpu.VMEM((FRAMES * ROWS * COLS // 2, 2 * CH), F32),
            pltpu.VMEM((FRAMES, ROWS, COLS, CH), F32),
            pltpu.VMEM((ROWS * COLS, FRAMES * 3 * CH), BF16),
            pltpu.VMEM((TAPS * CH, CH), F32),
            pltpu.VMEM((HALF, CH), F32),
            pltpu.VMEM((HALF, CH), F32),
            pltpu.VMEM((len(PLANED), plane, PIECE, CH), F32),
            pltpu.VMEM((len(PLANED), line, PIECE, CH), F32),
            pltpu.VMEM((len(LINED), line, STRIP, CH), F32),
            pltpu.VMEM((len(LINED), plane, STRIP, CH), F32),
            dma((5,)), dma((4,)), dma((ROWS,)), dma((6,)), dma, dma((5,)), dma((PARTS,)),
            dma((PARTS,)), dma((PARTS,)), dma((PARTS,)), dma,
        ],
        compiler_params=pltpu.CompilerParams(
            collective_id=0, has_side_effects=True, vmem_limit_bytes=48 << 20
        ),
        name="tokenizer_step",
    )(
        *(pltpu.with_memory_space_constraint(x, pltpu.HBM) for x in (
            latent[0], target[0], w_dec.reshape(2, 9 * CH, CH), w_disc.reshape(9 * CH, CH),
            w_head.reshape(1, CH), w_perc,
        ))
    )
    pixels = lax.axis_size("dp") * FRAMES * ROWS * lax.axis_size("sect") * COLS
    total = total / jnp.sqrt(jnp.float32(pixels))
    return total.reshape(2, 3, 3, CH, CH)


def solution(mesh):
    in_specs = (
        P("dp", None, "sect", None, None),
        P("dp", None, "sect", None, None),
        P(),
        P(),
        P(),
        P(),
    )
    return jax.shard_map(
        per_device, mesh=mesh, in_specs=in_specs, out_specs=P(), check_vma=False
    )
```
